32 devices in a mesh: group: 2 (over core), tensor: 16 (over z, y, x).
Axes of the slice: x: 2, y: 2, z: 4, core: 2. Of those that a mesh axis runs over, the one named last changes fastest.
Arguments:
- resid_in: bfloat16 [2, 256, 2880], P('group', 'tensor'), may hold values from -8 to 8
- queries: bfloat16 [2, 256, 4096], P('group', None, 'tensor'), may hold values from -100 to 100
- suffix_kv: bfloat16 [2, 256, 1024], P('group', 'tensor'), may hold values from -12 to 12
- prefix_kv: bfloat16 [2, 512, 1024], P('group', 'tensor'), may hold values from -7.1875 to 7.1875
- block_map: int32 [2, 16], P('group', 'tensor'), may hold values from 0 to 15, each once within a row
- lengths: int32 [2, 2], P('group'), may hold values from 1 to 128, as said below
- sinks: float32 [64], P('tensor'), may hold values from 7 to 12
- w_out: bfloat16 [4096, 2880], P('tensor'), may hold values from -1 to 1
- mlp_gain: float32 [2880], replicated, may hold values from 1 to 6
- routes: int32 [256, 2, 4], P('tensor'), may hold values from 0 to 31, all different within a row; in each aligned block of 32 rows (0 to 31, 32 to 63, ..., all dimensions but the last counted through in order) at most 8 rows name the same one
- w_experts: bfloat16 [32, 2880, 5760], P(('group', 'tensor')), may hold values from -0.109375 to 0.109375
Outputs:
- resid_out: bfloat16 [2, 256, 2880], P('group', 'tensor')
- expert_hidden: bfloat16 [32, 16, 8, 2880], P(('group', 'tensor'))
The draws below stay inside these ranges and needn't reach their ends.
Inputs may be any that keep to these rules, and one draw needn't show every extreme that they name: `lengths`: each group has one request of exactly 128 slots. `block_map`: each group's row is a permutation of the 16 block numbers. `routes`: each token names 4 different experts. Within one aligned block of slots (c * 16 to c * 16 + 15, all groups) no expert is named more than 8 times, a bound that some block reaches.
All inputs are finite; a program needn't handle non-finite values.
Results may differ from the reference program's by a relative error of at most 0.025.
Values may be sent and summed in bfloat16 or wider, within the bound.
No kernel may reach another device: no remote copies, remote signals or barrier semaphores. Data moves between devices by JAX's collectives and lax.ppermute only.
A program may use at most 128 MiB of HBM per device.

```python
import math
import jax
import jax.numpy as jnp
import numpy as np
from jax import lax

D = 2880
HEADS = 64
KVH = 8
HD = 64
EXPERTS = 32
TOPK = 4
REQS = 2
MAXLEN = 128
PBLK = 32
SLOTS = 256
TOK_DEV = 16
PREFIX = 512
PIECES = 32
PPE = 1
COPIES = 1
PFF = 2880
ROUTE_CAP = 8
SLOT_CAP = 8
N_GROUP = 2
N_TENSOR = 16


def draw_resid_in(key, part):
    key_base, key_rows, key_cols = jax.random.split(jax.random.fold_in(key, 11), 3)
    draw_shape = (N_GROUP, SLOTS, D)
    base_draw = jnp.clip(jax.random.normal(key_base, draw_shape, jnp.float32), -5.0, 5.0)
    row_scale = jnp.exp(jax.random.uniform(key_rows, (N_GROUP, SLOTS, 1), jnp.float32, 0.0, 1.15))
    col_scale = jnp.exp(jax.random.uniform(key_cols, (1, 1, D), jnp.float32, 0.0, 1.15))
    return (0.15 * base_draw * row_scale * col_scale).astype(jnp.bfloat16)


def draw_queries(key, part):
    key_base = jax.random.fold_in(jax.random.fold_in(key, 23), 0)
    draw_shape = (N_GROUP, SLOTS, HEADS * HD)
    base_draw = jnp.clip(jax.random.normal(key_base, draw_shape, jnp.float32), -6.0, 6.0)
    return (1.4 * base_draw).astype(jnp.bfloat16)


def draw_lengths(key, part):
    key_values, key_spot = jax.random.split(jax.random.fold_in(key, 37), 2)
    values = jax.random.randint(key_values, (N_GROUP, REQS), 1, MAXLEN + 1)
    full_spot = jax.random.randint(key_spot, (N_GROUP, 1), 0, REQS)
    return jnp.where(jnp.arange(REQS)[None, :] == full_spot, MAXLEN, values).astype(jnp.int32)


def shard_levels(key, dims, shards, least, high):
    gain, own = 1.0, jax.random.fold_in(key, 6)
    for position, blocks in shards:
        heights = jnp.exp(jax.random.uniform(jax.random.fold_in(own, position), (blocks,), jnp.float32, least / len(shards), high / len(shards)))
        gain = gain * jnp.repeat(heights, dims[position] // blocks).reshape([-1 if axis == position else 1 for axis in range(len(dims))])
    return gain


def routed_block(key, own, number, rows, count, top, reach, skew):
    order = jax.random.permutation(key, count)
    packed, ordinary = load_shares(count, rows * top, reach, skew, True), load_shares(count, rows * top, reach, skew, False)
    places = jnp.arange(count)

    def named(sizes, rotation):
        used = int((sizes > 0).sum())
        fixed = max(1, used // 4)
        moved = fixed + (places - fixed + rotation * (used - fixed)) % max(1, count - fixed)
        return jnp.zeros((count,), jnp.int32).at[order[jnp.where(places < fixed, places, moved)]].set(jnp.asarray(sizes, jnp.int32))

    sizes = jnp.where(number % 4 == 0, named(packed, number // 4), named(ordinary, number - number // 4 - 1))
    mixed = jax.random.permutation(jax.random.fold_in(own, 3), count)
    source_of, receiver = mixed[0:count // 2 * 2:2], mixed[1:count // 2 * 2:2]
    margin = jnp.minimum(sizes[source_of] - 1, reach - sizes[receiver]) // 2
    margin = jnp.where((source_of == order[0]) | (receiver == order[0]) | (sizes[receiver] == 0), 0, jnp.maximum(margin, 0))
    moved = jax.random.randint(jax.random.fold_in(own, 4), (count // 2,), 0, 1 << 20) % (margin + 1)
    sizes = sizes.at[source_of].add(-moved).at[receiver].add(moved)
    items = jnp.searchsorted(jnp.cumsum(sizes), jnp.arange(rows * top), side="right").astype(jnp.int32)
    listing = items.reshape(top, rows).T
    listing = listing[jax.random.permutation(jax.random.fold_in(own, 1), rows)]
    rotation = jax.random.randint(jax.random.fold_in(own, 2), (rows, 1), 0, top)
    return jnp.take_along_axis(listing, (jnp.arange(top)[None, :] + rotation) % top, axis=1)


def load_shares(count, total, bound, slope, full):
    portions = [(1 << 20) // math.isqrt(rank ** slope) + 1 for rank in range(1, count + 1)]
    largest = bound if full else min(bound, max(-(-total // count), total * portions[0] // sum(portions)))
    least = 1 if total - largest >= count - 1 else 0
    holding, surplus = [largest] + [least] * (count - 1), total - largest - least * (count - 1)
    while surplus > 0:
        free = [i for i in range(1, count) if holding[i] < largest] or [i for i in range(1, count) if holding[i] < bound]
        mass, remaining = sum([portions[i] for i in free]), surplus
        for i in free:
            more = min(bound - holding[i], max(1, remaining * portions[i] // mass), surplus)
            holding[i] = holding[i] + more
            surplus = surplus - more
    return np.array(holding)


def noise(rng, shape, width, reach, pieces=(), kind=jnp.bfloat16):
    values = jax.random.normal(rng, shape, jnp.float32) * width
    if len(pieces) > 0:
        values = shard_levels(rng, shape, pieces, -0.22, 0.18) * values
    return jnp.clip(values, min=-reach, max=reach).astype(kind)


def setup_inputs(seed: int = 0) -> dict:
    arg_keys = jax.random.split(jax.random.key(seed), 12)
    resid_in = draw_resid_in(jax.random.fold_in(arg_keys[11], 71), 0)
    queries = draw_queries(jax.random.fold_in(arg_keys[11], 71), 0)
    suffix_kv = noise(arg_keys[2], (N_GROUP, SLOTS, 2 * KVH * HD), 2.0, 12.0, ((0, 2), (1, 16)))
    prefix_kv = noise(arg_keys[3], (N_GROUP, PREFIX, 2 * KVH * HD), 1.2, 7.1875, ((0, 2), (1, 16)))
    block_map = jax.vmap(lambda own: jax.random.permutation(own, N_TENSOR))(jax.random.split(arg_keys[4], N_GROUP)).reshape((N_GROUP, N_TENSOR)).astype(jnp.int32)
    lengths = draw_lengths(jax.random.fold_in(arg_keys[11], 71), 0)
    sinks = jnp.clip(7.0 + 5.0 * jax.random.uniform(arg_keys[6], (HEADS,), jnp.float32) ** shard_levels(arg_keys[6], (HEADS,), ((0, 16),), -0.2, 0.2), 7.0, 12.0)
    w_out = noise(arg_keys[7], (HEADS * HD, D), (HD // 2) ** -0.5, 1.0, ((0, 16),))
    mlp_gain = jnp.clip(jnp.exp(jax.random.uniform(arg_keys[8], (D,), jnp.float32, math.log(1.0), math.log(6.0))), 1.0, 6.0)
    routes_keys = jax.random.split(jax.random.fold_in(arg_keys[9], 1), SLOTS * N_GROUP // (TOK_DEV * N_GROUP))
    routes_turns = jax.random.permutation(jax.random.fold_in(arg_keys[9], 3), SLOTS * N_GROUP // (TOK_DEV * N_GROUP))
    routes = jax.vmap(lambda own, number: routed_block(jax.random.fold_in(arg_keys[9], 2), own, number, TOK_DEV * N_GROUP, EXPERTS, TOPK, ROUTE_CAP, 2))(routes_keys, routes_turns).reshape((SLOTS, N_GROUP, TOPK))
    w_experts = noise(arg_keys[10], (PIECES, D, 2 * PFF), D ** -0.5, 0.109375, ((0, 32),))
    return {"resid_in": resid_in, "queries": queries, "suffix_kv": suffix_kv, "prefix_kv": prefix_kv, "block_map": block_map, "lengths": lengths, "sinks": sinks, "w_out": w_out, "mlp_gain": mlp_gain, "routes": routes, "w_experts": w_experts}


def rotate(values, positions):
    half_width = HD // 2
    frequency = jnp.power(150000.0, -2.0 * jnp.arange(half_width, dtype=jnp.float32) / HD)
    angles = positions[:, None] * frequency[None, :]
    cosine = jnp.cos(angles)[:, None, :]
    sine_part = jnp.sin(angles)[:, None, :]
    first_half = values[..., :half_width]
    second = values[..., half_width:]
    return jnp.concatenate([first_half * cosine - second * sine_part, second * cosine + first_half * sine_part], axis=-1)

def attend(group_queries, group_suffix, group_prefix, group_blocks, group_lengths, sinks):
    slot_ids = jnp.arange(SLOTS)
    slot_pos = (PREFIX + slot_ids % MAXLEN).astype(jnp.float32)
    row_ids = jnp.arange(PREFIX)
    prefix_pos = (jnp.take(group_blocks, row_ids // PBLK) * PBLK + row_ids % PBLK).astype(jnp.float32)
    repeat = HEADS // KVH
    query_rot = rotate(group_queries.astype(jnp.float32).reshape(SLOTS, HEADS, HD), slot_pos).astype(jnp.bfloat16)
    query_f = lax.optimization_barrier(query_rot).astype(jnp.float32).reshape(SLOTS, KVH, repeat, HD)
    suffix = group_suffix.reshape(SLOTS, 2, KVH, HD)
    key_rot = rotate(suffix[:, 0].astype(jnp.float32), slot_pos).astype(jnp.bfloat16)
    key_rot = lax.optimization_barrier(key_rot).astype(jnp.float32)
    suffix_vals = suffix[:, 1].astype(jnp.float32)
    prefix = group_prefix.reshape(PREFIX, 2, KVH, HD)
    prefix_keys = rotate(prefix[:, 0].astype(jnp.float32), prefix_pos).astype(jnp.bfloat16)
    prefix_keys = lax.optimization_barrier(prefix_keys).astype(jnp.float32)
    prefix_vals = prefix[:, 1].astype(jnp.float32)

    def one_block(block_pair):
        key_block, value_block = block_pair
        scores = 0.125 * jnp.einsum('sgrd,pgd->grsp', query_f, key_block)
        block_max = lax.optimization_barrier(jnp.max(scores, axis=-1))
        weights = jnp.exp(scores - block_max[..., None])
        total_sum = lax.optimization_barrier(jnp.sum(weights, axis=-1))
        rounded = lax.optimization_barrier(weights.astype(jnp.bfloat16)).astype(jnp.float32)
        mixed_sum = jnp.einsum('grsp,pgd->grsd', rounded, value_block)
        return (block_max, total_sum, mixed_sum)
    block_maxes, block_sums, block_mixes = lax.map(one_block, (prefix_keys.reshape(N_TENSOR, PBLK, KVH, HD), prefix_vals.reshape(N_TENSOR, PBLK, KVH, HD)))
    request = slot_ids // MAXLEN
    within = slot_ids % MAXLEN
    live_len = jnp.take(group_lengths, request)
    visible = (request[:, None] == request[None, :]) & (slot_ids[None, :] <= slot_ids[:, None]) & (within[None, :] < live_len[None, :])
    scores = 0.125 * jnp.einsum('sgrd,tgd->grst', query_f, key_rot)
    masked = jnp.where(visible, scores, -1e+30)
    suffix_max = lax.optimization_barrier(jnp.max(masked, axis=-1))
    weights = jnp.where(visible, jnp.exp(masked - suffix_max[..., None]), 0.0)
    suffix_sum = lax.optimization_barrier(jnp.sum(weights, axis=-1))
    rounded = lax.optimization_barrier(weights.astype(jnp.bfloat16)).astype(jnp.float32)
    suffix_mix = jnp.einsum('grst,tgd->grsd', rounded, suffix_vals)
    sink_logit = sinks.reshape(KVH, repeat)[:, :, None]
    overall_max = jnp.maximum(jnp.maximum(sink_logit, suffix_max), lax.optimization_barrier(jnp.max(block_maxes, axis=0)))
    suffix_scale = jnp.exp(suffix_max - overall_max)
    block_scales = jnp.exp(block_maxes - overall_max[None])
    denominator = jnp.exp(sink_logit - overall_max) + suffix_sum * suffix_scale + lax.optimization_barrier(jnp.sum(block_sums * block_scales, axis=0))
    numerator = suffix_mix * suffix_scale[..., None] + lax.optimization_barrier(jnp.sum(block_mixes * block_scales[..., None], axis=0))
    combined = numerator / denominator[..., None]
    return jnp.transpose(combined, (2, 0, 1, 3)).reshape(SLOTS, HEADS * HD).astype(jnp.bfloat16)

def reference(resid_in, queries, suffix_kv, prefix_kv, block_map, lengths, sinks, w_out, mlp_gain, routes, w_experts):
    results = []
    for group_index in range(N_GROUP):
        attended = attend(queries[group_index], suffix_kv[group_index], prefix_kv[group_index], block_map[group_index], lengths[group_index], sinks)
        projected = jnp.dot(attended, w_out, preferred_element_type=jnp.float32)
        results.append((resid_in[group_index].astype(jnp.float32) + projected).astype(jnp.bfloat16))
    resid_out = jnp.stack(results)
    widened = resid_out.astype(jnp.float32)
    normed = (widened * lax.rsqrt(lax.optimization_barrier(jnp.mean(widened * widened, axis=-1, keepdims=True)) + 1e-05) * mlp_gain).astype(jnp.bfloat16)
    flat_rows = normed.reshape(N_GROUP * SLOTS, D)
    pair_count = TOK_DEV * N_GROUP * TOPK
    named_experts = routes.reshape(N_TENSOR, pair_count)
    pair_ids = jnp.arange(pair_count)
    local_slot = pair_ids // (N_GROUP * TOPK)
    pair_group = pair_ids // TOPK % N_GROUP
    pair_row = pair_group[None, :] * SLOTS + jnp.arange(N_TENSOR)[:, None] * TOK_DEV + local_slot[None, :]
    onehot = (named_experts[:, :, None] == jnp.arange(EXPERTS)[None, None, :]).astype(jnp.int32)
    pair_rank = lax.optimization_barrier(jnp.sum((jnp.cumsum(onehot, axis=1) - 1) * onehot, axis=-1))
    matches = (named_experts[:, None, None, :] == jnp.arange(EXPERTS)[None, :, None, None]) & (pair_rank[:, None, None, :] == jnp.arange(ROUTE_CAP)[None, None, :, None])
    chosen = lax.optimization_barrier(jnp.sum(jnp.where(matches, pair_row[:, None, None, :], 0), axis=-1)).astype(jnp.int32)
    filled = jnp.any(matches, axis=-1)
    slot_rows = jnp.where(filled[..., None], jnp.take(flat_rows, chosen, axis=0), jnp.zeros((), jnp.bfloat16))
    tensor_copies = N_TENSOR // COPIES

    def one_piece(piece_item):
        piece_index, piece_weights = piece_item
        column = piece_index % N_TENSOR
        distinct = piece_index // N_TENSOR * tensor_copies + column % tensor_copies
        expert = (distinct // PPE).astype(jnp.int32)
        copy_index = (column // tensor_copies).astype(jnp.int32)
        row_block = jnp.take(slot_rows, expert, axis=1).reshape(N_TENSOR, SLOT_CAP, COPIES, D)
        row_block = jnp.take(row_block, copy_index, axis=2).reshape(N_TENSOR * SLOT_CAP, D)
        projected = jnp.dot(row_block, piece_weights, preferred_element_type=jnp.float32)
        gate_part = jnp.minimum(projected[:, :PFF], 7.0)
        up_part = jnp.clip(projected[:, PFF:], -7.0, 7.0)
        activated = (up_part + 1.0) * gate_part * jax.nn.sigmoid(1.702 * gate_part)
        return activated.astype(jnp.bfloat16).reshape(N_TENSOR, SLOT_CAP, PFF)
    expert_hidden = lax.map(one_piece, (jnp.arange(PIECES).astype(jnp.int32), w_experts))
    return (resid_out, expert_hidden)
```

```python
import functools

import jax
import jax.numpy as jnp
import numpy as np
from jax import lax
from jax.experimental import pallas as pl
from jax.experimental.pallas import tpu as pltpu
from jax.sharding import PartitionSpec as P

HEADS = 64
KVH = 8
HD = 64
EXPERTS = 32
MAXLEN = 128
LANES = 128
F32 = jnp.float32
BF16 = jnp.bfloat16
VMEM = pl.BlockSpec(memory_space=pltpu.VMEM)
SMEM = pl.BlockSpec(memory_space=pltpu.SMEM)
ANY = pl.BlockSpec(memory_space=pl.ANY)


def call(kernel, outs, specs, name, scratch=(), limit=48, flops=0, moved=0):
    single = not isinstance(outs, (list, tuple))
    return pl.pallas_call(
        kernel,
        out_shape=outs,
        in_specs=list(specs),
        out_specs=VMEM if single else [VMEM] * len(outs),
        scratch_shapes=list(scratch),
        name=name,
        compiler_params=pltpu.CompilerParams(vmem_limit_bytes=limit * 1024 * 1024),
        cost_estimate=pl.CostEstimate(flops=flops, bytes_accessed=moved, transcendentals=0),
    )


def rope_rows():
    lane = np.arange(LANES) % HD
    frequency = np.power(np.float32(150000.0), -2.0 * (lane % (HD // 2)) / HD).astype(np.float32)
    sign = np.where(lane < HD // 2, -1.0, 1.0).astype(np.float32)
    return np.stack([frequency, sign])


def partner(values):
    lane = lax.broadcasted_iota(jnp.int32, values.shape, 1)
    ahead = pltpu.roll(values, LANES - HD // 2, 1)
    behind = pltpu.roll(values, HD // 2, 1)
    return jnp.where(lane % HD < HD // 2, ahead, behind)


def prep_kernel(heads_here, tensors, place_ref, rope_ref, suffix_ref, prefix_ref, out_ref):
    block_rows = prefix_ref.shape[0]
    tok_dev = suffix_ref.shape[0]
    prefix_len = block_rows * tensors
    half = KVH * HD

    def part(ref, first, low):
        rows = ref.shape[0]
        row = lax.broadcasted_iota(jnp.int32, (rows, LANES), 0) + first
        angle = row.astype(F32) * rope_ref[0:1, :]
        cosine = jnp.cos(angle)
        sine = jnp.sin(angle) * rope_ref[1:2, :]
        lane = lax.broadcasted_iota(jnp.int32, (rows, LANES), 1)
        for pair in range(KVH // 2):
            span = slice(pair * LANES, (pair + 1) * LANES)
            keys = ref[:, span].astype(F32)
            vals = ref[:, slice(half + pair * LANES, half + (pair + 1) * LANES)].astype(F32)
            turned = keys * cosine + partner(keys) * sine
            both = (
                jnp.where(lane < HD, turned, pltpu.roll(vals, HD, 1)).astype(BF16),
                jnp.where(lane < HD, pltpu.roll(turned, HD, 1), vals).astype(BF16),
            )
            for peer in range(tensors):
                head = peer * heads_here // (HEADS // KVH)
                if head // 2 == pair:
                    out_ref[peer, low : low + rows, :] = both[head % 2]

    part(prefix_ref, place_ref[0], 0)
    part(suffix_ref, prefix_len + place_ref[1] % MAXLEN, block_rows)


def attend_kernel(
    pairs, halves, len_ref, sink_ref, cos_ref, sin_ref, slot_ref, q_ref, kv_ref, w_ref, out_ref, att_ref
):
    kv = kv_ref[...].astype(F32)
    swapped = pltpu.roll(kv, HD, 1)
    low = lax.broadcasted_iota(jnp.int32, kv.shape, 1) < HD
    keys = jnp.where(low, kv, swapped).astype(BF16)
    vals = jnp.where(low, swapped, kv).astype(BF16)
    key_slot = slot_ref[...]
    cosine = cos_ref[...]
    sine = sin_ref[...]
    lane_low = lax.broadcasted_iota(jnp.int32, (MAXLEN, LANES), 1) < HD
    for req in range(q_ref.shape[0] // MAXLEN):
        base = req * MAXLEN
        rows = slice(base, base + MAXLEN)
        row = lax.broadcasted_iota(jnp.int32, (MAXLEN, 1), 0) + base
        last = jnp.minimum(row, base + len_ref[req] - 1)
        visible = (key_slot < 0) | ((key_slot >= base) & (key_slot <= last))
        for pair in range(pairs):
            span = slice(pair * LANES, (pair + 1) * LANES)
            query = q_ref[rows, span].astype(F32)
            query = (query * cosine + partner(query) * sine).astype(BF16).astype(F32) * 0.125
            mixed = []
            for half in range(halves):
                mine = jnp.where(lane_low if half == 0 else ~lane_low, query, 0.0).astype(BF16)
                scores = lax.dot_general(
                    mine, keys, (((1,), (1,)), ((), ())), preferred_element_type=F32
                )
                scores = jnp.where(visible, scores, -1e30)
                sink = sink_ref[pair * halves + half]
                top = jnp.maximum(jnp.max(scores, axis=1, keepdims=True), sink)
                weights = jnp.exp(scores - top)
                total = jnp.sum(weights, axis=1, keepdims=True) + jnp.exp(sink - top)
                got = jnp.dot(weights.astype(BF16), vals, preferred_element_type=F32)
                mixed.append(got / total)
            if halves == 2:
                value = jnp.where(lane_low, mixed[0], mixed[1])
            else:
                value = jnp.where(lane_low, mixed[0], 0.0)
            att_ref[rows, span] = value.astype(BF16)
    out_ref[...] = jnp.dot(att_ref[...], w_ref[...], preferred_element_type=F32).astype(BF16)


def norm_kernel(parts_ref, resid_ref, gain_ref, out_ref, normed_ref):
    total = parts_ref[0].astype(F32)
    for peer in range(1, parts_ref.shape[0]):
        total = total + parts_ref[peer].astype(F32)
    rounded = (resid_ref[...].astype(F32) + total).astype(BF16)
    out_ref[...] = rounded
    wide = rounded.astype(F32)
    scale = lax.rsqrt(jnp.mean(wide * wide, axis=1, keepdims=True) + 1e-05)
    normed_ref[...] = (wide * scale * gain_ref[...]).astype(BF16)


def dispatch_kernel(names_ref, want_ref, earlier_ref, source_ref, rows_ref, out_ref):
    pairs = names_ref.shape[1]
    expert = lax.broadcasted_iota(jnp.int32, (EXPERTS, pairs), 0)
    onehot = (names_ref[...] == expert).astype(F32)
    rank = jnp.dot(onehot.astype(BF16), earlier_ref[...], preferred_element_type=F32)
    pair_rank = jnp.sum(rank * onehot, axis=0, keepdims=True).astype(jnp.int32)
    slots = out_ref.shape[0]
    wanted = want_ref[...]
    picked = (names_ref[...] == wanted[:, 0:1]) & (pair_rank == wanted[:, 1:2])
    chosen = jnp.dot(picked.astype(F32).astype(BF16), source_ref[...], preferred_element_type=F32)
    out_ref[...] = jnp.dot(
        chosen.astype(BF16), rows_ref[...], preferred_element_type=F32
    ).astype(BF16)


def expert_kernel(bounds, rows_ref, w_ref, out_ref, held, total, sems):
    copies = [
        pltpu.make_async_copy(w_ref.at[pl.ds(lo, hi - lo)], held.at[pl.ds(lo, hi - lo)], sems.at[k])
        for k, (lo, hi) in enumerate(bounds)
    ]
    for copy in copies:
        copy.start()
    for k, (lo, hi) in enumerate(bounds):
        copies[k].wait()
        part = jnp.dot(rows_ref[:, lo:hi], held[lo:hi, :], preferred_element_type=F32)
        if k == 0:
            total[...] = part
        else:
            total[...] += part
    width = out_ref.shape[1]
    gate = jnp.minimum(total[:, :width], 7.0)
    up = jnp.clip(total[:, width : 2 * width], -7.0, 7.0)
    out_ref[...] = ((up + 1.0) * gate / (1.0 + jnp.exp(-1.702 * gate))).astype(BF16)


def local(
    resid_in,
    queries,
    suffix_kv,
    prefix_kv,
    block_map,
    lengths,
    sinks,
    w_out,
    mlp_gain,
    routes,
    w_experts,
):
    groups = lax.axis_size("group")
    tensors = lax.axis_size("tensor")
    me_group = lax.axis_index("group")
    me_tensor = lax.axis_index("tensor")
    block_rows = prefix_kv.shape[1]
    prefix_len = block_rows * tensors
    slot_count = queries.shape[1]
    heads_here = queries.shape[2] // HD
    tok_dev = resid_in.shape[1]
    width = resid_in.shape[2]

    rope = rope_rows()
    place = jnp.stack([block_map[0, 0] * block_rows, me_tensor * tok_dev]).astype(jnp.int32)
    kv_rows = block_rows + tok_dev
    owned = call(
        functools.partial(prep_kernel, heads_here, tensors),
        jax.ShapeDtypeStruct((tensors, kv_rows, LANES), BF16),
        [SMEM, VMEM, VMEM, VMEM],
        "rotate_keys",
    )(place, jnp.asarray(rope), suffix_kv[0], prefix_kv[0])
    kv = lax.all_to_all(owned, "tensor", split_axis=0, concat_axis=0, tiled=True)
    kv = kv.reshape(tensors * kv_rows, LANES)

    halves = min(heads_here, 2)
    pairs = heads_here // halves
    flat_queries = queries[0]
    weights = w_out
    if halves == 1:
        flat_queries = jnp.pad(flat_queries, ((0, 0), (0, LANES - HD)))
        weights = jnp.pad(weights, ((0, LANES - HD), (0, 0)))
    angle = (prefix_len + np.arange(MAXLEN)).astype(np.float32)[:, None] * rope[0][None, :]
    cosine = np.cos(angle).astype(np.float32)
    sine = (np.sin(angle) * rope[1][None, :]).astype(np.float32)
    row_ids = np.arange(tensors * kv_rows)
    inside = row_ids % kv_rows - block_rows
    key_slot = np.where(inside < 0, -1, row_ids // kv_rows * tok_dev + inside).astype(np.int32)
    parts = call(
        functools.partial(attend_kernel, pairs, halves),
        jax.ShapeDtypeStruct((slot_count, width), BF16),
        [SMEM, SMEM] + [VMEM] * 6,
        "attend_project",
        scratch=[pltpu.VMEM((slot_count, pairs * LANES), BF16)],
    )(
        lengths[0],
        sinks,
        jnp.asarray(cosine),
        jnp.asarray(sine),
        jnp.asarray(key_slot[None, :]),
        flat_queries,
        kv,
        weights,
    )
    parts = lax.all_to_all(
        parts.reshape(tensors, tok_dev, width), "tensor", split_axis=0, concat_axis=0, tiled=True
    )
    resid_out, normed = call(
        norm_kernel,
        [jax.ShapeDtypeStruct((tok_dev, width), BF16)] * 2,
        [VMEM] * 3,
        "sum_norm",
    )(parts, resid_in[0], mlp_gain[None, :])

    flat_rows = lax.all_gather(normed, "group", axis=0, tiled=True)
    top_count = routes.shape[2]
    pair_count = tok_dev * groups * top_count
    pair_ids = np.arange(pair_count)
    pair_row = pair_ids // top_count % groups * tok_dev + pair_ids // (groups * top_count)
    source = (pair_row[:, None] == np.arange(groups * tok_dev)[None, :]).astype(np.float32)
    earlier = (pair_ids[:, None] < pair_ids[None, :]).astype(np.float32)
    pieces_total = groups * tensors
    pieces_each = min(8, pieces_total // EXPERTS)
    copies = pieces_total // (EXPERTS * pieces_each)
    tensor_copies = tensors // copies
    slot_cap = pair_count // 16 // copies
    slot = np.arange(tensors * slot_cap)
    peer = slot // slot_cap
    expert = (me_group * tensor_copies + peer % tensor_copies) // pieces_each
    rank = slot % slot_cap * copies + peer // tensor_copies
    want = jnp.stack([expert.astype(jnp.int32), jnp.asarray(rank, jnp.int32)], axis=1)
    outgoing = call(
        dispatch_kernel,
        jax.ShapeDtypeStruct((tensors * slot_cap, width), BF16),
        [VMEM] * 5,
        "dispatch",
    )(
        routes.reshape(1, pair_count),
        want,
        jnp.asarray(earlier, BF16),
        jnp.asarray(source, BF16),
        flat_rows,
    )
    arrived = lax.all_to_all(
        outgoing.reshape(tensors, slot_cap, width),
        "tensor",
        split_axis=0,
        concat_axis=0,
        tiled=True,
    )
    piece = w_experts[0]
    columns = piece.shape[1]
    step = 384
    bounds = [(lo, min(lo + step, width)) for lo in range(0, width, step)]
    hidden = call(
        functools.partial(expert_kernel, bounds),
        jax.ShapeDtypeStruct((tensors * slot_cap, columns // 2), BF16),
        [VMEM, ANY],
        "experts",
        scratch=[
            pltpu.VMEM((width, columns), BF16),
            pltpu.VMEM((tensors * slot_cap, columns), F32),
            pltpu.SemaphoreType.DMA((len(bounds),)),
        ],
        limit=56,
    )(arrived.reshape(tensors * slot_cap, width), piece)
    return (resid_out[None], hidden.reshape(1, tensors, slot_cap, columns // 2))


def solution(mesh):
    placed = (
        P("group", "tensor", None),
        P("group", None, "tensor"),
        P("group", "tensor", None),
        P("group", "tensor", None),
        P("group", "tensor"),
        P("group", None),
        P("tensor"),
        P("tensor", None),
        P(),
        P("tensor", None, None),
        P(("group", "tensor"), None, None),
    )
    return jax.shard_map(
        local,
        mesh=mesh,
        in_specs=placed,
        out_specs=(P("group", "tensor", None), P(("group", "tensor"), None, None, None)),
        check_vma=False,
    )
```

```python
import functools
import math

import jax
import jax.numpy as jnp
import numpy as np
from jax import lax
from jax.experimental import pallas as pl
from jax.experimental.pallas import tpu as pltpu
from jax.sharding import PartitionSpec as P

HEADS = 64
KVH = 8
HD = 64
EXPERTS = 32
MAXLEN = 128
LANES = 128
F32 = jnp.float32
BF16 = jnp.bfloat16
VMEM = pl.BlockSpec(memory_space=pltpu.VMEM)
SMEM = pl.BlockSpec(memory_space=pltpu.SMEM)
ANY = pl.BlockSpec(memory_space=pl.ANY)
PLANE = 4


def call(kernel, outs, specs, name, scratch=(), limit=12, moved=0, space=VMEM):
    single = not isinstance(outs, (list, tuple))
    return pl.pallas_call(
        kernel,
        out_shape=outs,
        in_specs=list(specs),
        out_specs=space if single else [space] * len(outs),
        scratch_shapes=list(scratch),
        name=name,
        compiler_params=pltpu.CompilerParams(vmem_limit_bytes=limit * 1024 * 1024),
        cost_estimate=pl.CostEstimate(flops=0, bytes_accessed=moved, transcendentals=0),
    )


def log2(number):
    assert number & (number - 1) == 0
    return number.bit_length() - 1


def rope_rows():
    lane = np.arange(LANES) % HD
    frequency = np.power(np.float32(150000.0), -2.0 * (lane % (HD // 2)) / HD).astype(np.float32)
    sign = np.where(lane < HD // 2, -1.0, 1.0).astype(np.float32)
    return np.stack([frequency, sign])


def partner(values):
    lane = lax.broadcasted_iota(jnp.int32, values.shape, 1)
    ahead = pltpu.roll(values, LANES - HD // 2, 1)
    behind = pltpu.roll(values, HD // 2, 1)
    return jnp.where(lane % HD < HD // 2, ahead, behind)


def keys_kernel(heads_here, tensors, block_ref, suffix_ref, prefix_ref, out_ref):
    block_rows = prefix_ref.shape[0]
    tok_dev = suffix_ref.shape[0]
    prefix_len = block_rows * tensors
    half = KVH * HD
    share = HEADS // KVH

    def part(ref, first, low):
        rows = ref.shape[0]
        row = lax.broadcasted_iota(jnp.int32, (rows, LANES), 0) + first
        lane = lax.broadcasted_iota(jnp.int32, (1, LANES), 1) & (HD - 1)
        exponent = (lane & (HD // 2 - 1)).astype(F32) * (-2.0 * math.log(150000.0) / HD)
        angle = row.astype(F32) * jnp.exp(exponent)
        cosine = jnp.cos(angle)
        sine = jnp.sin(angle) * jnp.where(lane < HD // 2, -1.0, 1.0)
        left = lax.broadcasted_iota(jnp.int32, (rows, LANES), 1) < HD
        made = {}
        for peer in range(tensors):
            one = peer * heads_here // share
            two = (peer ^ 2) * heads_here // share
            if (one, two) not in made:
                pair = one // 2
                keys = ref[:, pair * LANES : (pair + 1) * LANES].astype(F32)
                vals = ref[:, half + pair * LANES : half + (pair + 1) * LANES].astype(F32)
                turned = keys * cosine + partner(keys) * sine

                def ordered(values):
                    swapped = pltpu.roll(values, HD, 1)
                    first_half = values if one % 2 == 0 else swapped
                    second_half = values if two % 2 == 1 else swapped
                    return jnp.where(left, first_half, second_half).astype(BF16)

                made[one, two] = ordered(turned), ordered(vals)
            out_ref[peer, low : low + rows, :LANES] = made[one, two][0]
            out_ref[peer, low : low + rows, LANES:] = made[one, two][1]

    part(prefix_ref, block_ref[0, 0] * block_rows, 0)
    part(suffix_ref, prefix_len + lax.axis_index("tensor") * tok_dev % MAXLEN, block_rows)


def queries_kernel(tok_dev, sink_ref, turn_ref, q_ref, *out_refs):
    me = lax.axis_index("tensor")
    planes = q_ref.shape[0] // tok_dev // PLANE
    width = q_ref.shape[1]
    lane = lax.broadcasted_iota(jnp.int32, (16, width), 1)
    row = lax.broadcasted_iota(jnp.int32, (16, width), 0)
    sink = jnp.zeros((16, width), F32)
    for head in range(width // HD):
        sink = jnp.where((lane >= head * HD) & (lane < head * HD + HD), sink_ref[head], sink)
    high = sink.astype(BF16).astype(F32)
    middle = (sink - high).astype(BF16).astype(F32)
    low = sink - high - middle
    terms = jnp.where(row == 0, high, jnp.where(row == 1, middle, jnp.where(row == 2, low, 0.0)))
    for peer in range(PLANE):
        for plane in range(planes):
            block = me ^ (plane * PLANE + peer)
            rows = pl.ds(pl.multiple_of(block * tok_dev, tok_dev), tok_dev)
            turn = block * tok_dev % MAXLEN
            cosine = turn_ref[pl.ds(pl.multiple_of(turn, tok_dev), tok_dev), :]
            sine = turn_ref[pl.ds(pl.multiple_of(turn + MAXLEN, tok_dev), tok_dev), :]
            for pair in range(width // LANES):
                span = slice(pair * LANES, (pair + 1) * LANES)
                query = q_ref[rows, span].astype(F32)
                turned = query * cosine + partner(query) * sine
                out_refs[peer][plane * tok_dev : (plane + 1) * tok_dev, span] = turned.astype(BF16)
        out_refs[peer][planes * tok_dev : planes * tok_dev + 16, :] = terms.astype(BF16)


def rotate_kernel(turn_ref, q_ref, out_ref):
    for req in range(q_ref.shape[0] // MAXLEN):
        rows = slice(req * MAXLEN, (req + 1) * MAXLEN)
        query = q_ref[rows, :].astype(F32)
        turned = query * turn_ref[:MAXLEN] + partner(query) * turn_ref[MAXLEN:]
        out_ref[rows, :] = turned.astype(BF16)


def attend_kernel(blocks, tok_dev, kv_rows, len_ref, *refs):
    q_refs, kv_ref, resid_refs, out_ref = refs[:blocks], refs[blocks], refs[blocks + 1 : -1], refs[-1]
    rows = q_refs[0].shape[0] - 16
    inner = lax.axis_index("tensor") & (PLANE - 1)
    plane = lax.axis_index("tensor") >> log2(PLANE)
    low = lax.broadcasted_iota(jnp.int32, (kv_ref.shape[0], LANES), 1) < HD

    def doubled(values):
        swapped = pltpu.roll(values, HD, 1)
        return (
            jnp.where(low, values, swapped).astype(BF16),
            jnp.where(low, swapped, values).astype(BF16),
        )

    keys = doubled(kv_ref[:, :LANES].astype(F32))
    vals = doubled(kv_ref[:, LANES:].astype(F32))
    row = lax.broadcasted_iota(jnp.int32, (2 * rows, 1), 0)
    row = row & (rows - 1)
    shift = tok_dev.bit_length() - 1
    slot = (((row >> shift) ^ plane) * PLANE + inner) * tok_dev + (row & (tok_dev - 1))
    request = slot >> (MAXLEN.bit_length() - 1)
    length = jnp.zeros_like(slot)
    for number in range(len_ref.shape[1]):
        length = jnp.where(request == number, len_ref[0, number], length)
    base = request * MAXLEN
    last = jnp.minimum(slot, base + length - 1)
    key_row = lax.broadcasted_iota(jnp.int32, (1, kv_ref.shape[0]), 1)
    source = jnp.floor((key_row.astype(F32) + 0.5) * (1.0 / kv_rows)).astype(jnp.int32)
    inside = key_row - source * kv_rows - (kv_rows - tok_dev)
    key_slot = jnp.where(inside < 0, -1, source * tok_dev + inside)
    visible = (key_slot < 0) | ((key_slot >= base) & (key_slot <= last))
    left = lax.broadcasted_iota(jnp.int32, (rows, LANES), 1) < HD
    for block in range(blocks):
        for pair in range(2):
            half = block // 2 if blocks == PLANE else pair
            span = slice(pair * LANES, (pair + 1) * LANES)
            query = q_refs[block][:rows, span].astype(F32) * 0.125
            stack = jnp.concatenate(
                [jnp.where(left, query, 0.0), jnp.where(left, 0.0, query)], axis=0
            ).astype(BF16)
            scores = lax.dot_general(
                stack, keys[half], (((1,), (1,)), ((), ())), preferred_element_type=F32
            )
            scores = jnp.where(visible, scores, -1e30)
            terms = q_refs[block][rows : rows + 16, span].astype(F32)
            sinks = terms[0:1] + terms[1:2] + terms[2:3]
            sink = jnp.concatenate(
                [
                    jnp.broadcast_to(sinks[:, 0:1], (rows, 1)),
                    jnp.broadcast_to(sinks[:, HD : HD + 1], (rows, 1)),
                ],
                axis=0,
            )
            top = jnp.maximum(jnp.max(scores, axis=1, keepdims=True), sink)
            weights = jnp.exp(scores - top)
            total = jnp.sum(weights, axis=1, keepdims=True) + jnp.exp(sink - top)
            got = jnp.dot(weights.astype(BF16), vals[half], preferred_element_type=F32) / total
            at = block * 2 * LANES + pair * LANES
            out_ref[:rows, at : at + LANES] = jnp.where(left, got[:rows], got[rows:]).astype(BF16)
    for resid_ref in resid_refs:
        step = out_ref.shape[1]
        for number, first in enumerate(range(0, resid_ref.shape[1], step)):
            size = min(step, resid_ref.shape[1] - first)
            at = rows + number * tok_dev
            out_ref[at : at + tok_dev, :size] = resid_ref[:, first : first + size]


def project_kernel(tok_dev, groups, att_ref, *refs):
    w_refs, out_refs = refs[: PLANE + 1], refs[PLANE + 1 :]
    depth = w_refs[0].shape[1]
    slots = att_ref.shape[0] // groups
    taken = out_refs[0].shape[0] * len(out_refs) // groups
    rows = jnp.concatenate(
        [att_ref[group * slots : group * slots + taken, :] for group in range(groups)], axis=0
    )

    def times(peer, w_ref):
        return lax.dot_general(
            rows[:, peer * depth : (peer + 1) * depth],
            w_ref[...],
            (((1,), (1,)), ((), ())),
            preferred_element_type=F32,
        )

    far = jnp.concatenate([times(3, w_refs[3]), times(3, w_refs[4])], axis=1)
    whole = times(0, w_refs[0]) + times(1, w_refs[1]) + times(2, w_refs[2]) + far
    slots = taken
    if len(out_refs) == 1:
        out_refs[0][...] = whole
        return
    for plane, out_ref in enumerate(out_refs):
        for group in range(groups):
            first = group * slots + plane * tok_dev
            out_ref[group * tok_dev : (group + 1) * tok_dev, :] = whole[
                first : first + tok_dev
            ].astype(out_ref.dtype)


def split_kernel(top_ref, bottom_ref, top_out, bottom_out, sems):
    first, last = top_out.shape[0], bottom_out.shape[0]
    copies = [
        pltpu.make_async_copy(top_ref.at[pl.ds(0, first)], top_out, sems.at[0]),
        pltpu.make_async_copy(bottom_ref.at[pl.ds(first, last)], bottom_out, sems.at[1]),
    ]
    for copy in copies:
        copy.start()
    for copy in copies:
        copy.wait()


def load_kernel(w_ref, out_ref, sem):
    copy = pltpu.make_async_copy(w_ref.at[pl.ds(0, out_ref.shape[0])], out_ref, sem)
    copy.start()
    copy.wait()


def sum_kernel(*refs):
    total = refs[0][...].astype(F32)
    for ref in refs[1:-1]:
        total = total + ref[...].astype(F32)
    refs[-1][...] = total


def dispatch_kernel(
    groups,
    slot_cap,
    tensor_copies,
    pieces_each,
    copies,
    names_ref,
    earlier_ref,
    source_ref,
    gain_ref,
    resid_ref,
    sums_ref,
    resid_out_ref,
    out_ref,
    held,
):
    rows = held.shape[0]
    tok_dev = rows // groups
    width = sums_ref.shape[1]
    for part in range(groups):
        held[:, part * width : (part + 1) * width] = sums_ref[part * rows : (part + 1) * rows, :]
    if resid_ref.shape == held.shape:
        resid = resid_ref[...].astype(F32)
    else:
        each = resid_ref.shape[0] // groups
        step = resid_ref.shape[1]
        count = -(-held.shape[1] // step)
        first = each - count * tok_dev
        resid = jnp.concatenate(
            [
                jnp.concatenate(
                    [
                        resid_ref[
                            group * each + first + number * tok_dev :
                            group * each + first + (number + 1) * tok_dev,
                            : min(step, held.shape[1] - number * step),
                        ].astype(F32)
                        for number in range(count)
                    ],
                    axis=1,
                )
                for group in range(groups)
            ],
            axis=0,
        )
    rounded = (resid + held[...]).astype(BF16)
    wide = rounded.astype(F32)
    own = wide[:tok_dev]
    me_group = lax.axis_index("group")
    for group in range(1, groups):
        own = jnp.where(
            me_group == group, wide[group * tok_dev : (group + 1) * tok_dev], own
        )
    resid_out_ref[...] = own.astype(BF16)
    scale = lax.rsqrt(jnp.mean(wide * wide, axis=1, keepdims=True) + 1e-05)
    normed = (wide * scale * gain_ref[...]).astype(BF16)

    pairs = names_ref.shape[1]
    expert = lax.broadcasted_iota(jnp.int32, (EXPERTS, pairs), 0)
    onehot = (names_ref[...] == expert).astype(F32)
    rank = jnp.dot(onehot.astype(BF16), earlier_ref[...], preferred_element_type=F32)
    pair_rank = jnp.sum(rank * onehot, axis=0, keepdims=True).astype(jnp.int32)
    slot = lax.broadcasted_iota(jnp.int32, (out_ref.shape[0], 1), 0)
    peer = slot >> log2(slot_cap)
    piece = me_group * tensor_copies + (peer & (tensor_copies - 1))
    wanted_rank = (slot & (slot_cap - 1)) * copies + (peer >> log2(tensor_copies))
    picked = (names_ref[...] == piece >> log2(pieces_each)) & (pair_rank == wanted_rank)
    chosen = jnp.dot(picked.astype(F32).astype(BF16), source_ref[...], preferred_element_type=F32)
    out_ref[...] = jnp.dot(chosen.astype(BF16), normed, preferred_element_type=F32).astype(BF16)


def expert_kernel(bounds, rows_ref, early_ref, w_ref, out_ref, held, total, sems):
    start = early_ref.shape[0]
    copies = [
        pltpu.make_async_copy(
            w_ref.at[pl.ds(lo, hi - lo)], held.at[pl.ds(lo - start, hi - lo)], sems.at[k]
        )
        for k, (lo, hi) in enumerate(bounds)
    ]
    for copy in copies:
        copy.start()
    total[...] = jnp.dot(rows_ref[:, :start], early_ref[...], preferred_element_type=F32)
    for k, (lo, hi) in enumerate(bounds):
        copies[k].wait()
        total[...] += jnp.dot(
            rows_ref[:, lo:hi], held[lo - start : hi - start, :], preferred_element_type=F32
        )
    width = out_ref.shape[1]
    gate = jnp.minimum(total[:, :width], 7.0)
    up = jnp.clip(total[:, width : 2 * width], -7.0, 7.0)
    out_ref[...] = ((up + 1.0) * gate / (1.0 + jnp.exp(-1.702 * gate))).astype(BF16)


def local(
    resid_in,
    queries,
    suffix_kv,
    prefix_kv,
    block_map,
    lengths,
    sinks,
    w_out,
    mlp_gain,
    routes,
    w_experts,
):
    groups = lax.axis_size("group")
    tensors = lax.axis_size("tensor")
    me_group = lax.axis_index("group")
    me_tensor = lax.axis_index("tensor")
    block_rows = prefix_kv.shape[1]
    prefix_len = block_rows * tensors
    slot_count = queries.shape[1]
    heads_here = queries.shape[2] // HD
    tok_dev = resid_in.shape[1]
    width = resid_in.shape[2]
    planes = tensors // PLANE
    slots_here = planes * tok_dev
    aligned = tok_dev % 16 == 0 and heads_here % 2 == 0

    def swap(values, bits):
        return lax.ppermute(values, "tensor", [(i, i ^ bits) for i in range(tensors)])

    columns_here = width // groups
    cut = columns_here // 2
    held = lax.dynamic_slice_in_dim(w_out.T, me_group * columns_here, columns_here, 0)
    beside, across = swap(held, 1), swap(held, 2)

    kv_rows = block_rows + tok_dev
    rope = rope_rows()
    angle = (prefix_len + np.arange(MAXLEN)).astype(np.float32)[:, None] * rope[0][None, :]
    turns = np.concatenate([np.cos(angle), np.sin(angle) * rope[1][None, :]], axis=0)
    turns = jnp.asarray(turns.astype(np.float32))
    query_cols = heads_here * HD
    top_count = routes.shape[2]
    pair_count = tok_dev * groups * top_count

    def exchange(suffix, prefix, mine, sink_logits, block, named, gains):
        owned = call(
            functools.partial(keys_kernel, heads_here, tensors),
            jax.ShapeDtypeStruct((tensors, kv_rows, 2 * LANES), BF16),
            [SMEM, VMEM, VMEM],
            "rotate_keys",
        )(block, suffix, prefix)
        kv = lax.all_to_all(owned, "tensor", split_axis=0, concat_axis=0, tiled=True)
        if aligned:
            sent = call(
                functools.partial(queries_kernel, tok_dev),
                [jax.ShapeDtypeStruct((slots_here + 16, query_cols), BF16)] * PLANE,
                [SMEM, VMEM, VMEM],
                "rotate_queries",
            )(sink_logits, turns, mine)
        else:
            padded = jnp.pad(mine, ((0, 0), (0, LANES - query_cols)))
            turned = call(
                rotate_kernel,
                jax.ShapeDtypeStruct(padded.shape, BF16),
                [VMEM, VMEM],
                "rotate_queries",
            )(turns, padded)[:, :query_cols]
            turned = turned.reshape(tensors, tok_dev, query_cols)
            turned = jnp.take(turned, me_tensor ^ jnp.arange(tensors), axis=0)
            turned = turned.reshape(planes, PLANE, tok_dev, query_cols)
            spread = jnp.repeat(sink_logits, HD)
            high = lax.reduce_precision(spread, 8, 7)
            middle = lax.reduce_precision(spread - high, 8, 7)
            terms = jnp.pad(jnp.stack([high, middle, spread - high - middle]), ((0, 13), (0, 0)))
            sent = [
                jnp.concatenate(
                    [turned[:, peer].reshape(slots_here, query_cols), terms.astype(BF16)], axis=0
                )
                for peer in range(PLANE)
            ]
        moved = [swap(sent[peer], peer) for peer in range(1, PLANE)]
        return (kv, named.reshape(1, pair_count), gains[None, :], sent[0], *moved)

    def nothing(*operands):
        shape = (slots_here + 16, query_cols)
        kv = jnp.zeros((tensors, kv_rows, 2 * LANES), BF16)
        names, gain = jnp.zeros((1, pair_count), jnp.int32), jnp.zeros((1, width), F32)
        return (kv, names, gain, *(jnp.zeros(shape, BF16) for _ in range(PLANE)))

    kv, names, gain, *received = lax.cond(
        lengths[0, 0] > 0,
        exchange,
        nothing,
        suffix_kv[0],
        prefix_kv[0],
        queries[0],
        sinks,
        block_map,
        routes,
        mlp_gain,
    )
    kv, beside, across = lax.optimization_barrier((kv, beside, across))
    halves = call(
        split_kernel,
        [
            jax.ShapeDtypeStruct((cut, held.shape[1]), BF16),
            jax.ShapeDtypeStruct((columns_here - cut, held.shape[1]), BF16),
        ],
        [ANY, ANY],
        "split",
        scratch=[pltpu.SemaphoreType.DMA((2,))],
        limit=2,
        space=ANY,
    )(beside, across)
    far = [swap(halves[0], 2), swap(halves[1], 1)]
    projections = [held, beside, across, *far]
    kv = kv.reshape(tensors * kv_rows, 2 * LANES)
    if not aligned:
        received = [jnp.concatenate(received, axis=1)]

    packed = [resid_in[0]] if aligned else []
    extra = -(-width // (PLANE * query_cols)) * tok_dev if aligned else 0
    attended = call(
        functools.partial(attend_kernel, len(received), tok_dev, kv_rows),
        jax.ShapeDtypeStruct((slots_here + extra, PLANE * query_cols), BF16),
        [SMEM] + [VMEM] * (1 + len(received) + int(aligned)),
        "attend",
    )(lengths, *received, kv, *packed)

    attended = lax.all_gather(attended, "group", axis=0, tiled=True)
    rows_here = groups * tok_dev
    if aligned:
        outs = [
            jax.ShapeDtypeStruct((rows_here, columns_here), F32 if plane == 0 else BF16)
            for plane in range(planes)
        ]
    else:
        outs = [jax.ShapeDtypeStruct((groups * slots_here, columns_here), F32)]
    parts = call(
        functools.partial(project_kernel, tok_dev, groups),
        outs,
        [VMEM] * (2 + PLANE),
        "project",
    )(attended, *projections)
    if not aligned:
        split = parts[0].reshape(groups, planes, tok_dev, columns_here)
        parts = [split[:, plane].reshape(rows_here, columns_here) for plane in range(planes)]
        parts = [parts[0]] + [part.astype(BF16) for part in parts[1:]]
    pair_ids = np.arange(pair_count)
    pair_row = pair_ids // top_count % groups * tok_dev + pair_ids // (groups * top_count)
    source = (pair_row[:, None] == np.arange(groups * tok_dev)[None, :]).astype(np.float32)
    earlier = (pair_ids[:, None] < pair_ids[None, :]).astype(np.float32)
    pieces_total = groups * tensors
    pieces_each = min(8, pieces_total // EXPERTS)
    copies = pieces_total // (EXPERTS * pieces_each)
    tensor_copies = tensors // copies
    slot_cap = pair_count // 16 // copies
    resid_all = attended if aligned else lax.all_gather(resid_in[0], "group", axis=0, tiled=True)
    *parts, piece = lax.optimization_barrier((*parts, w_experts[0]))
    arrived = [parts[0]] + [swap(parts[plane], plane * PLANE) for plane in range(1, planes)]
    columns = piece.shape[1]
    step = 384
    early_rows = 5 * step
    early = call(
        load_kernel,
        jax.ShapeDtypeStruct((early_rows, columns), BF16),
        [ANY],
        "load_expert",
        scratch=[pltpu.SemaphoreType.DMA],
        limit=12,
        moved=2 * early_rows * columns * 2,
    )(piece)
    *arrived, early = lax.optimization_barrier((*arrived, early))
    sums = call(
        sum_kernel,
        jax.ShapeDtypeStruct((rows_here, columns_here), F32),
        [VMEM] * planes,
        "sum_planes",
    )(*arrived)
    sums = lax.all_gather(sums, "group", axis=0, tiled=True)

    resid_out, outgoing = call(
        functools.partial(
            dispatch_kernel, groups, slot_cap, tensor_copies, pieces_each, copies
        ),
        [
            jax.ShapeDtypeStruct((tok_dev, width), BF16),
            jax.ShapeDtypeStruct((tensors * slot_cap, width), BF16),
        ],
        [VMEM] * 6,
        "norm_dispatch",
        scratch=[pltpu.VMEM((rows_here, width), F32)],
    )(
        names,
        jnp.asarray(earlier, BF16),
        jnp.asarray(source, BF16),
        gain,
        resid_all,
        sums,
    )
    rows = lax.all_to_all(
        outgoing.reshape(tensors, slot_cap, width),
        "tensor",
        split_axis=0,
        concat_axis=0,
        tiled=True,
    )
    bounds = [(lo, min(lo + step, width)) for lo in range(early_rows, width, step)]
    hidden = call(
        functools.partial(expert_kernel, bounds),
        jax.ShapeDtypeStruct((tensors * slot_cap, columns // 2), BF16),
        [VMEM, VMEM, ANY],
        "experts",
        scratch=[
            pltpu.VMEM((width - early_rows, columns), BF16),
            pltpu.VMEM((tensors * slot_cap, columns), F32),
            pltpu.SemaphoreType.DMA((len(bounds),)),
        ],
        limit=24,
    )(rows.reshape(tensors * slot_cap, width), early, piece)
    return (resid_out[None], hidden.reshape(1, tensors, slot_cap, columns // 2))


def solution(mesh):
    placed = (
        P("group", "tensor", None),
        P("group", None, "tensor"),
        P("group", "tensor", None),
        P("group", "tensor", None),
        P("group", "tensor"),
        P("group", None),
        P("tensor"),
        P("tensor", None),
        P(),
        P("tensor", None, None),
        P(("group", "tensor"), None, None),
    )
    return jax.shard_map(
        local,
        mesh=mesh,
        in_specs=placed,
        out_specs=(P("group", "tensor", None), P(("group", "tensor"), None, None, None)),
        check_vma=False,
    )
```

```python
import functools
import math

import jax
import jax.numpy as jnp
import numpy as np
from jax import lax
from jax.experimental import pallas as pl
from jax.experimental.pallas import tpu as pltpu
from jax.sharding import PartitionSpec as P

HEADS = 64
KVH = 8
HD = 64
EXPERTS = 32
MAXLEN = 128
LANES = 128
F32 = jnp.float32
BF16 = jnp.bfloat16
VMEM = pl.BlockSpec(memory_space=pltpu.VMEM)
SMEM = pl.BlockSpec(memory_space=pltpu.SMEM)
ANY = pl.BlockSpec(memory_space=pl.ANY)
PLANE = 4


def call(kernel, outs, specs, name, scratch=(), limit=12, moved=0, space=VMEM, flops=0):
    single = not isinstance(outs, (list, tuple))
    return pl.pallas_call(
        kernel,
        out_shape=outs,
        in_specs=list(specs),
        out_specs=space if single else [space] * len(outs),
        scratch_shapes=list(scratch),
        name=name,
        compiler_params=pltpu.CompilerParams(vmem_limit_bytes=limit * 1024 * 1024),
        cost_estimate=pl.CostEstimate(flops=flops, bytes_accessed=moved, transcendentals=0),
    )


def log2(number):
    assert number & (number - 1) == 0
    return number.bit_length() - 1


def rope_rows():
    lane = np.arange(LANES) % HD
    frequency = np.power(np.float32(150000.0), -2.0 * (lane % (HD // 2)) / HD).astype(np.float32)
    sign = np.where(lane < HD // 2, -1.0, 1.0).astype(np.float32)
    return np.stack([frequency, sign])


def partner(values):
    lane = lax.broadcasted_iota(jnp.int32, values.shape, 1)
    ahead = pltpu.roll(values, LANES - HD // 2, 1)
    behind = pltpu.roll(values, HD // 2, 1)
    return jnp.where(lane % HD < HD // 2, ahead, behind)


def keys_kernel(
    heads_here, tensors, block_ref, suffix_hbm, prefix_hbm, out_ref, suffix_ref, prefix_ref, sems
):
    copies = [
        pltpu.make_async_copy(prefix_hbm, prefix_ref, sems.at[0]),
        pltpu.make_async_copy(suffix_hbm, suffix_ref, sems.at[1]),
    ]
    for copy in copies:
        copy.start()
    block_rows = prefix_ref.shape[0]
    tok_dev = suffix_ref.shape[0]
    prefix_len = block_rows * tensors
    half = KVH * HD
    share = HEADS // KVH

    def part(ref, first, low):
        rows = ref.shape[0]
        row = lax.broadcasted_iota(jnp.int32, (rows, LANES), 0) + first
        lane = lax.broadcasted_iota(jnp.int32, (1, LANES), 1) & (HD - 1)
        exponent = (lane & (HD // 2 - 1)).astype(F32) * (-2.0 * math.log(150000.0) / HD)
        angle = row.astype(F32) * jnp.exp(exponent)
        cosine = jnp.cos(angle)
        sine = jnp.sin(angle) * jnp.where(lane < HD // 2, -1.0, 1.0)
        left = lax.broadcasted_iota(jnp.int32, (rows, LANES), 1) < HD
        made = {}
        for peer in range(tensors):
            one = peer * heads_here // share
            two = (peer ^ 2) * heads_here // share
            if (one, two) not in made:
                pair = one // 2
                keys = ref[:, pair * LANES : (pair + 1) * LANES].astype(F32)
                vals = ref[:, half + pair * LANES : half + (pair + 1) * LANES].astype(F32)
                turned = keys * cosine + partner(keys) * sine

                def ordered(values):
                    swapped = pltpu.roll(values, HD, 1)
                    first_half = values if one % 2 == 0 else swapped
                    second_half = values if two % 2 == 1 else swapped
                    return jnp.where(left, first_half, second_half).astype(BF16)

                made[one, two] = ordered(turned), ordered(vals)
            out_ref[peer, low : low + rows, :LANES] = made[one, two][0]
            out_ref[peer, low : low + rows, LANES:] = made[one, two][1]

    copies[0].wait()
    part(prefix_ref, block_ref[0, 0] * block_rows, 0)
    copies[1].wait()
    part(suffix_ref, prefix_len + lax.axis_index("tensor") * tok_dev % MAXLEN, block_rows)


def queries_kernel(tok_dev, len_ref, sink_ref, turn_ref, q_ref, resid_ref, *out_refs):
    me = lax.axis_index("tensor")
    planes = q_ref.shape[0] // tok_dev // PLANE
    width = q_ref.shape[1]
    lane = lax.broadcasted_iota(jnp.int32, (16, width), 1)
    row = lax.broadcasted_iota(jnp.int32, (16, width), 0)
    sink = jnp.zeros((16, width), F32)
    for head in range(width // HD):
        sink = jnp.where((lane >= head * HD) & (lane < head * HD + HD), sink_ref[head], sink)
    high = sink.astype(BF16).astype(F32)
    middle = (sink - high).astype(BF16).astype(F32)
    low = sink - high - middle
    terms = jnp.where(row == 0, high, jnp.where(row == 1, middle, jnp.where(row == 2, low, 0.0)))
    for number in range(len_ref.shape[1]):
        terms = jnp.where(row == 3 + number, len_ref[0, number].astype(F32), terms)
    for peer in range(PLANE):
        for plane in range(planes):
            block = me ^ (plane * PLANE + peer)
            rows = pl.ds(pl.multiple_of(block * tok_dev, tok_dev), tok_dev)
            turn = block * tok_dev % MAXLEN
            cosine = turn_ref[pl.ds(pl.multiple_of(turn, tok_dev), tok_dev), :]
            sine = turn_ref[pl.ds(pl.multiple_of(turn + MAXLEN, tok_dev), tok_dev), :]
            for pair in range(width // LANES):
                span = slice(pair * LANES, (pair + 1) * LANES)
                query = q_ref[rows, span].astype(F32)
                turned = query * cosine + partner(query) * sine
                out_refs[peer][plane * tok_dev : (plane + 1) * tok_dev, span] = turned.astype(BF16)
        out_refs[peer][planes * tok_dev : planes * tok_dev + 16, :] = terms.astype(BF16)
    step = out_refs[-1].shape[1]
    for number, first in enumerate(range(0, resid_ref.shape[1], step)):
        size = min(step, resid_ref.shape[1] - first)
        rows = slice(number * tok_dev, (number + 1) * tok_dev)
        out_refs[-1][rows, :size] = resid_ref[:, first : first + size]


def rotate_kernel(turn_ref, q_ref, out_ref):
    for req in range(q_ref.shape[0] // MAXLEN):
        rows = slice(req * MAXLEN, (req + 1) * MAXLEN)
        query = q_ref[rows, :].astype(F32)
        turned = query * turn_ref[:MAXLEN] + partner(query) * turn_ref[MAXLEN:]
        out_ref[rows, :] = turned.astype(BF16)


def attend_kernel(blocks, requests, tok_dev, kv_rows, *refs):
    q_refs, kv_ref, w_ref = refs[:blocks], refs[blocks], refs[blocks + 1]
    resid_refs, (out_ref, early_ref, own_ref, sems) = refs[blocks + 2 : -4], refs[-4:]
    own = pltpu.make_async_copy(q_refs[0], own_ref, sems.at[0])
    own.start()
    rows = own_ref.shape[0] - 16
    loads = [
        pltpu.make_async_copy(resid_ref, out_ref.at[pl.ds(rows, resid_ref.shape[0])], sems.at[1])
        for resid_ref in resid_refs
    ]
    loads.append(
        pltpu.make_async_copy(w_ref.at[pl.ds(0, early_ref.shape[0])], early_ref, sems.at[2])
    )
    for load in loads:
        load.start()
    q_refs = [own_ref, *q_refs[1:]]
    told_ref = q_refs[-1]
    if blocks == 1:
        own.wait()
    inner = lax.axis_index("tensor") & (PLANE - 1)
    plane = lax.axis_index("tensor") >> log2(PLANE)
    low = lax.broadcasted_iota(jnp.int32, (kv_ref.shape[0], LANES), 1) < HD

    def doubled(values):
        swapped = pltpu.roll(values, HD, 1)
        return (
            jnp.where(low, values, swapped).astype(BF16),
            jnp.where(low, swapped, values).astype(BF16),
        )

    keys = doubled(kv_ref[:, :LANES].astype(F32))
    vals = doubled(kv_ref[:, LANES:].astype(F32))
    row = lax.broadcasted_iota(jnp.int32, (2 * rows, 1), 0)
    row = row & (rows - 1)
    shift = tok_dev.bit_length() - 1
    slot = (((row >> shift) ^ plane) * PLANE + inner) * tok_dev + (row & (tok_dev - 1))
    request = slot >> (MAXLEN.bit_length() - 1)
    length = jnp.zeros_like(slot)
    told = told_ref[rows : rows + 16, :LANES].astype(F32)
    for number in range(requests):
        live = told[3 + number : 4 + number, 0:1].astype(jnp.int32)
        length = jnp.where(request == number, live, length)
    base = request * MAXLEN
    last = jnp.minimum(slot, base + length - 1)
    key_row = lax.broadcasted_iota(jnp.int32, (1, kv_ref.shape[0]), 1)
    source = jnp.floor((key_row.astype(F32) + 0.5) * (1.0 / kv_rows)).astype(jnp.int32)
    inside = key_row - source * kv_rows - (kv_rows - tok_dev)
    key_slot = jnp.where(inside < 0, -1, source * tok_dev + inside)
    visible = (key_slot < 0) | ((key_slot >= base) & (key_slot <= last))
    left = lax.broadcasted_iota(jnp.int32, (rows, LANES), 1) < HD
    for block in reversed(range(blocks)):
        if block == 0 and blocks > 1:
            own.wait()
        for pair in range(2):
            half = block // 2 if blocks == PLANE else pair
            span = slice(pair * LANES, (pair + 1) * LANES)
            query = q_refs[block][:rows, span].astype(F32) * 0.125
            stack = jnp.concatenate(
                [jnp.where(left, query, 0.0), jnp.where(left, 0.0, query)], axis=0
            ).astype(BF16)
            scores = lax.dot_general(
                stack, keys[half], (((1,), (1,)), ((), ())), preferred_element_type=F32
            )
            scores = jnp.where(visible, scores, -1e30)
            terms = q_refs[block][rows : rows + 16, span].astype(F32)
            sinks = terms[0:1] + terms[1:2] + terms[2:3]
            sink = jnp.concatenate(
                [
                    jnp.broadcast_to(sinks[:, 0:1], (rows, 1)),
                    jnp.broadcast_to(sinks[:, HD : HD + 1], (rows, 1)),
                ],
                axis=0,
            )
            top = jnp.maximum(jnp.max(scores, axis=1, keepdims=True), sink)
            weights = jnp.exp(scores - top)
            total = jnp.sum(weights, axis=1, keepdims=True) + jnp.exp(sink - top)
            got = jnp.dot(weights.astype(BF16), vals[half], preferred_element_type=F32) / total
            at = block * 2 * LANES + pair * LANES
            out_ref[:rows, at : at + LANES] = jnp.where(left, got[:rows], got[rows:]).astype(BF16)
    for load in loads:
        load.wait()


def project_kernel(tok_dev, groups, att_ref, *refs):
    w_refs, out_refs = refs[: PLANE + 1], refs[PLANE + 1 :]
    depth = w_refs[0].shape[1]
    slots = att_ref.shape[0] // groups
    taken = out_refs[0].shape[0] * len(out_refs) // groups
    rows = jnp.concatenate(
        [att_ref[group * slots : group * slots + taken, :] for group in range(groups)], axis=0
    )

    def times(peer, w_ref):
        return lax.dot_general(
            rows[:, peer * depth : (peer + 1) * depth],
            w_ref[...],
            (((1,), (1,)), ((), ())),
            preferred_element_type=F32,
        )

    far = jnp.concatenate([times(3, w_refs[3]), times(3, w_refs[4])], axis=1)
    whole = times(0, w_refs[0]) + times(1, w_refs[1]) + times(2, w_refs[2]) + far
    slots = taken
    if len(out_refs) == 1:
        out_refs[0][...] = whole
        return
    for plane, out_ref in enumerate(out_refs):
        for group in range(groups):
            first = group * slots + plane * tok_dev
            out_ref[group * tok_dev : (group + 1) * tok_dev, :] = whole[
                first : first + tok_dev
            ].astype(out_ref.dtype)


def split_kernel(top_ref, bottom_ref, top_out, bottom_out, sems):
    first, last = top_out.shape[0], bottom_out.shape[0]
    copies = [
        pltpu.make_async_copy(top_ref.at[pl.ds(0, first)], top_out, sems.at[0]),
        pltpu.make_async_copy(bottom_ref.at[pl.ds(first, last)], bottom_out, sems.at[1]),
    ]
    for copy in copies:
        copy.start()
    for copy in copies:
        copy.wait()


def load_kernel(w_ref, out_ref, sem):
    count = out_ref.shape[0]
    copy = pltpu.make_async_copy(w_ref.at[pl.ds(w_ref.shape[0] - count, count)], out_ref, sem)
    copy.start()
    copy.wait()


def sum_kernel(*refs):
    total = refs[0][...].astype(F32)
    for ref in refs[1:-1]:
        total = total + ref[...].astype(F32)
    refs[-1][...] = total


def dispatch_kernel(
    groups,
    slot_cap,
    tensor_copies,
    pieces_each,
    copies,
    names_ref,
    earlier_ref,
    source_ref,
    gain_ref,
    resid_ref,
    sums_ref,
    resid_out_ref,
    out_ref,
    held,
):
    rows = held.shape[0]
    tok_dev = rows // groups
    width = sums_ref.shape[1]
    for part in range(groups):
        held[:, part * width : (part + 1) * width] = sums_ref[part * rows : (part + 1) * rows, :]
    if resid_ref.shape == held.shape:
        resid = resid_ref[...].astype(F32)
    else:
        each = resid_ref.shape[0] // groups
        step = resid_ref.shape[1]
        count = -(-held.shape[1] // step)
        first = each - count * tok_dev
        resid = jnp.concatenate(
            [
                jnp.concatenate(
                    [
                        resid_ref[
                            group * each + first + number * tok_dev :
                            group * each + first + (number + 1) * tok_dev,
                            : min(step, held.shape[1] - number * step),
                        ].astype(F32)
                        for number in range(count)
                    ],
                    axis=1,
                )
                for group in range(groups)
            ],
            axis=0,
        )
    rounded = (resid + held[...]).astype(BF16)
    wide = rounded.astype(F32)
    own = wide[:tok_dev]
    me_group = lax.axis_index("group")
    for group in range(1, groups):
        own = jnp.where(
            me_group == group, wide[group * tok_dev : (group + 1) * tok_dev], own
        )
    resid_out_ref[...] = own.astype(BF16)
    scale = lax.rsqrt(jnp.mean(wide * wide, axis=1, keepdims=True) + 1e-05)
    normed = (wide * scale * gain_ref[...]).astype(BF16)

    pairs = names_ref.shape[1]
    expert = lax.broadcasted_iota(jnp.int32, (EXPERTS, pairs), 0)
    onehot = (names_ref[...] == expert).astype(F32)
    rank = jnp.dot(onehot.astype(BF16), earlier_ref[...], preferred_element_type=F32)
    pair_rank = jnp.sum(rank * onehot, axis=0, keepdims=True).astype(jnp.int32)
    slot = lax.broadcasted_iota(jnp.int32, (out_ref.shape[0], 1), 0)
    peer = slot >> log2(slot_cap)
    piece = me_group * tensor_copies + (peer & (tensor_copies - 1))
    wanted_rank = (slot & (slot_cap - 1)) * copies + (peer >> log2(tensor_copies))
    picked = (names_ref[...] == piece >> log2(pieces_each)) & (pair_rank == wanted_rank)
    chosen = jnp.dot(picked.astype(F32).astype(BF16), source_ref[...], preferred_element_type=F32)
    out_ref[...] = jnp.dot(chosen.astype(BF16), normed, preferred_element_type=F32).astype(BF16)


def expert_kernel(rows_ref, early_ref, late_ref, out_ref):
    start = early_ref.shape[0]
    width = out_ref.shape[1]
    total = jnp.dot(rows_ref[:, :start], early_ref[...], preferred_element_type=F32)
    total = total + jnp.dot(rows_ref[:, start:], late_ref[...], preferred_element_type=F32)
    gate = jnp.minimum(total[:, :width], 7.0)
    up = jnp.clip(total[:, width : 2 * width], -7.0, 7.0)
    out_ref[...] = ((up + 1.0) * gate / (1.0 + jnp.exp(-1.702 * gate))).astype(BF16)


def local(
    resid_in,
    queries,
    suffix_kv,
    prefix_kv,
    block_map,
    lengths,
    sinks,
    w_out,
    mlp_gain,
    routes,
    w_experts,
):
    groups = lax.axis_size("group")
    tensors = lax.axis_size("tensor")
    me_group = lax.axis_index("group")
    me_tensor = lax.axis_index("tensor")
    block_rows = prefix_kv.shape[1]
    prefix_len = block_rows * tensors
    slot_count = queries.shape[1]
    heads_here = queries.shape[2] // HD
    tok_dev = resid_in.shape[1]
    width = resid_in.shape[2]
    planes = tensors // PLANE
    slots_here = planes * tok_dev
    aligned = tok_dev % 16 == 0 and heads_here % 2 == 0

    def swap(values, bits):
        return lax.ppermute(values, "tensor", [(i, i ^ bits) for i in range(tensors)])

    columns_here = width // groups
    cut = columns_here // 2
    held = lax.dynamic_slice_in_dim(w_out.T, me_group * columns_here, columns_here, 0)
    beside, across = swap(held, 1), swap(held, 2)

    kv_rows = block_rows + tok_dev
    rope = rope_rows()
    angle = (prefix_len + np.arange(MAXLEN)).astype(np.float32)[:, None] * rope[0][None, :]
    turns = np.concatenate([np.cos(angle), np.sin(angle) * rope[1][None, :]], axis=0)
    turns = jnp.asarray(turns.astype(np.float32))
    query_cols = heads_here * HD
    top_count = routes.shape[2]
    pair_count = tok_dev * groups * top_count

    owned = call(
        functools.partial(keys_kernel, heads_here, tensors),
        jax.ShapeDtypeStruct((tensors, kv_rows, 2 * LANES), BF16),
        [SMEM, ANY, ANY],
        "rotate_keys",
        scratch=[
            pltpu.VMEM(suffix_kv.shape[1:], BF16),
            pltpu.VMEM(prefix_kv.shape[1:], BF16),
            pltpu.SemaphoreType.DMA((2,)),
        ],
    )(block_map, suffix_kv[0], prefix_kv[0])
    if aligned:
        extra = -(-width // (PLANE * query_cols)) * tok_dev
        *sent, packed = call(
            functools.partial(queries_kernel, tok_dev),
            [jax.ShapeDtypeStruct((slots_here + 16, query_cols), BF16)] * PLANE
            + [jax.ShapeDtypeStruct((extra, PLANE * query_cols), BF16)],
            [SMEM, SMEM, VMEM, VMEM, VMEM],
            "rotate_queries",
        )(lengths, sinks, turns, queries[0], resid_in[0])
        packed = [packed]
    else:
        extra, packed = 0, []
        padded = jnp.pad(queries[0], ((0, 0), (0, LANES - query_cols)))
        turned = call(
            rotate_kernel,
            jax.ShapeDtypeStruct(padded.shape, BF16),
            [VMEM, VMEM],
            "rotate_queries",
        )(turns, padded)[:, :query_cols]
        turned = turned.reshape(tensors, tok_dev, query_cols)
        turned = jnp.take(turned, me_tensor ^ jnp.arange(tensors), axis=0)
        turned = turned.reshape(planes, PLANE, tok_dev, query_cols)
        spread = jnp.repeat(sinks, HD)
        high = lax.reduce_precision(spread, 8, 7)
        middle = lax.reduce_precision(spread - high, 8, 7)
        told = jnp.broadcast_to(lengths[0].astype(F32)[:, None], (lengths.shape[1], query_cols))
        terms = jnp.concatenate([jnp.stack([high, middle, spread - high - middle]), told], axis=0)
        terms = jnp.pad(terms, ((0, 16 - terms.shape[0]), (0, 0))).astype(BF16)
        sent = [
            jnp.concatenate([turned[:, peer].reshape(slots_here, query_cols), terms], axis=0)
            for peer in range(PLANE)
        ]
    kv = lax.all_to_all(owned, "tensor", split_axis=0, concat_axis=0, tiled=True)
    received = [sent[0]] + [swap(sent[peer], peer) for peer in range(1, PLANE)]
    names, gain = routes.reshape(1, pair_count), mlp_gain[None, :]
    beside, across, names, gain = lax.optimization_barrier((beside, across, names, gain))
    halves = call(
        split_kernel,
        [
            jax.ShapeDtypeStruct((cut, held.shape[1]), BF16),
            jax.ShapeDtypeStruct((columns_here - cut, held.shape[1]), BF16),
        ],
        [ANY, ANY],
        "split",
        scratch=[pltpu.SemaphoreType.DMA((2,))],
        limit=2,
        space=ANY,
    )(beside, across)
    far = [swap(halves[0], 2), swap(halves[1], 1)]
    projections = [held, beside, across, *far]
    kv = kv.reshape(tensors * kv_rows, 2 * LANES)
    if not aligned:
        received = [jnp.concatenate(received, axis=1)]

    columns = w_experts.shape[2]
    early_rows = min(width // 2, 768)
    attended, early = call(
        functools.partial(attend_kernel, len(received), lengths.shape[1], tok_dev, kv_rows),
        [
            jax.ShapeDtypeStruct((slots_here + extra, PLANE * query_cols), BF16),
            jax.ShapeDtypeStruct((early_rows, columns), BF16),
        ],
        [ANY] + [VMEM] * len(received) + [ANY] * (1 + len(packed)),
        "attend",
        scratch=[
            pltpu.VMEM(received[0].shape, BF16),
            pltpu.SemaphoreType.DMA((3,)),
        ],
        limit=26,
        moved=15000000,
        flops=5000000000,
    )(*received, kv, w_experts[0], *packed)

    attended = lax.all_gather(attended, "group", axis=0, tiled=True)
    rows_here = groups * tok_dev
    if aligned:
        outs = [
            jax.ShapeDtypeStruct((rows_here, columns_here), F32 if plane == 0 else BF16)
            for plane in range(planes)
        ]
    else:
        outs = [jax.ShapeDtypeStruct((groups * slots_here, columns_here), F32)]
    parts = call(
        functools.partial(project_kernel, tok_dev, groups),
        outs,
        [VMEM] * (2 + PLANE),
        "project",
    )(attended, *projections)
    if not aligned:
        split = parts[0].reshape(groups, planes, tok_dev, columns_here)
        parts = [split[:, plane].reshape(rows_here, columns_here) for plane in range(planes)]
        parts = [parts[0]] + [part.astype(BF16) for part in parts[1:]]
    pair_ids = np.arange(pair_count)
    pair_row = pair_ids // top_count % groups * tok_dev + pair_ids // (groups * top_count)
    source = (pair_row[:, None] == np.arange(groups * tok_dev)[None, :]).astype(np.float32)
    earlier = (pair_ids[:, None] < pair_ids[None, :]).astype(np.float32)
    pieces_total = groups * tensors
    pieces_each = min(8, pieces_total // EXPERTS)
    copies = pieces_total // (EXPERTS * pieces_each)
    tensor_copies = tensors // copies
    slot_cap = pair_count // 16 // copies
    resid_all = attended if aligned else lax.all_gather(resid_in[0], "group", axis=0, tiled=True)
    *parts, piece = lax.optimization_barrier((*parts, w_experts[0]))
    arrived = [swap(parts[plane], plane * PLANE) for plane in reversed(range(1, planes))]
    arrived = [parts[0]] + arrived
    late = call(
        load_kernel,
        jax.ShapeDtypeStruct((width - early_rows, columns), BF16),
        [ANY],
        "load_expert",
        scratch=[pltpu.SemaphoreType.DMA],
        limit=4,
        moved=2 * (width - early_rows) * columns * 2,
    )(piece)
    *arrived, late = lax.optimization_barrier((*arrived, late))
    sums = call(
        sum_kernel,
        jax.ShapeDtypeStruct((rows_here, columns_here), F32),
        [VMEM] * planes,
        "sum_planes",
    )(*arrived)
    sums = lax.all_gather(sums, "group", axis=0, tiled=True)

    resid_out, outgoing = call(
        functools.partial(
            dispatch_kernel, groups, slot_cap, tensor_copies, pieces_each, copies
        ),
        [
            jax.ShapeDtypeStruct((tok_dev, width), BF16),
            jax.ShapeDtypeStruct((tensors * slot_cap, width), BF16),
        ],
        [VMEM] * 6,
        "norm_dispatch",
        scratch=[pltpu.VMEM((rows_here, width), F32)],
    )(
        names,
        jnp.asarray(earlier, BF16),
        jnp.asarray(source, BF16),
        gain,
        resid_all,
        sums,
    )
    rows = lax.all_to_all(
        outgoing.reshape(tensors, slot_cap, width),
        "tensor",
        split_axis=0,
        concat_axis=0,
        tiled=True,
    )
    hidden = call(
        expert_kernel,
        jax.ShapeDtypeStruct((tensors * slot_cap, columns // 2), BF16),
        [VMEM] * 3,
        "experts",
        limit=16,
    )(rows.reshape(tensors * slot_cap, width), early, late)
    return (resid_out[None], hidden.reshape(1, tensors, slot_cap, columns // 2))


def solution(mesh):
    placed = (
        P("group", "tensor", None),
        P("group", None, "tensor"),
        P("group", "tensor", None),
        P("group", "tensor", None),
        P("group", "tensor"),
        P("group", None),
        P("tensor"),
        P("tensor", None),
        P(),
        P("tensor", None, None),
        P(("group", "tensor"), None, None),
    )
    return jax.shard_map(
        local,
        mesh=mesh,
        in_specs=placed,
        out_specs=(P("group", "tensor", None), P(("group", "tensor"), None, None, None)),
        check_vma=False,
    )
```

```python
import functools
import math

import jax
import jax.numpy as jnp
import numpy as np
from jax import lax
from jax.experimental import pallas as pl
from jax.experimental.pallas import tpu as pltpu
from jax.sharding import PartitionSpec as P

HEADS = 64
KVH = 8
HD = 64
EXPERTS = 32
MAXLEN = 128
LANES = 128
F32 = jnp.float32
BF16 = jnp.bfloat16
VMEM = pl.BlockSpec(memory_space=pltpu.VMEM)
SMEM = pl.BlockSpec(memory_space=pltpu.SMEM)
ANY = pl.BlockSpec(memory_space=pl.ANY)
PLANE = 4


def call(kernel, outs, specs, name, scratch=(), limit=12, moved=0, space=VMEM, flops=0):
    single = not isinstance(outs, (list, tuple))
    return pl.pallas_call(
        kernel,
        out_shape=outs,
        in_specs=list(specs),
        out_specs=space if single else [space] * len(outs),
        scratch_shapes=list(scratch),
        name=name,
        compiler_params=pltpu.CompilerParams(vmem_limit_bytes=int(limit * 1024 * 1024)),
        cost_estimate=pl.CostEstimate(flops=flops, bytes_accessed=moved, transcendentals=0),
    )


def log2(number):
    assert number & (number - 1) == 0
    return number.bit_length() - 1


def rope_rows():
    lane = np.arange(LANES) % HD
    frequency = np.power(np.float32(150000.0), -2.0 * (lane % (HD // 2)) / HD).astype(np.float32)
    sign = np.where(lane < HD // 2, -1.0, 1.0).astype(np.float32)
    return np.stack([frequency, sign])


def partner(values):
    lane = lax.broadcasted_iota(jnp.int32, values.shape, 1)
    ahead = pltpu.roll(values, LANES - HD // 2, 1)
    behind = pltpu.roll(values, HD // 2, 1)
    return jnp.where(lane % HD < HD // 2, ahead, behind)


def keys_kernel(
    heads_here, tensors, block_ref, suffix_hbm, prefix_hbm, out_ref, suffix_ref, prefix_ref, sems
):
    copies = [
        pltpu.make_async_copy(prefix_hbm, prefix_ref, sems.at[0]),
        pltpu.make_async_copy(suffix_hbm, suffix_ref, sems.at[1]),
    ]
    for copy in copies:
        copy.start()
    block_rows = prefix_ref.shape[0]
    tok_dev = suffix_ref.shape[0]
    prefix_len = block_rows * tensors
    half = KVH * HD
    share = HEADS // KVH

    def part(ref, first, low):
        rows = ref.shape[0]
        row = lax.broadcasted_iota(jnp.int32, (rows, LANES), 0) + first
        lane = lax.broadcasted_iota(jnp.int32, (1, LANES), 1) & (HD - 1)
        exponent = (lane & (HD // 2 - 1)).astype(F32) * (-2.0 * math.log(150000.0) / HD)
        angle = row.astype(F32) * jnp.exp(exponent)
        cosine = jnp.cos(angle)
        sine = jnp.sin(angle) * jnp.where(lane < HD // 2, -1.0, 1.0)
        left = lax.broadcasted_iota(jnp.int32, (rows, LANES), 1) < HD
        made = {}
        for peer in range(tensors):
            one = peer * heads_here // share
            two = (peer ^ 2) * heads_here // share
            if (one, two) not in made:
                pair = one // 2
                keys = ref[:, pair * LANES : (pair + 1) * LANES].astype(F32)
                vals = ref[:, half + pair * LANES : half + (pair + 1) * LANES].astype(F32)
                turned = keys * cosine + partner(keys) * sine

                def ordered(values):
                    swapped = pltpu.roll(values, HD, 1)
                    first_half = values if one % 2 == 0 else swapped
                    second_half = values if two % 2 == 1 else swapped
                    return jnp.where(left, first_half, second_half).astype(BF16)

                made[one, two] = ordered(turned), ordered(vals)
            out_ref[peer, low : low + rows, :LANES] = made[one, two][0]
            out_ref[peer, low : low + rows, LANES:] = made[one, two][1]

    copies[0].wait()
    part(prefix_ref, block_ref[0, 0] * block_rows, 0)
    copies[1].wait()
    part(suffix_ref, prefix_len + lax.axis_index("tensor") * tok_dev % MAXLEN, block_rows)


def queries_kernel(tok_dev, len_ref, sink_ref, turn_ref, q_ref, resid_ref, *out_refs):
    me = lax.axis_index("tensor")
    planes = q_ref.shape[0] // tok_dev // PLANE
    width = q_ref.shape[1]
    lane = lax.broadcasted_iota(jnp.int32, (16, width), 1)
    row = lax.broadcasted_iota(jnp.int32, (16, width), 0)
    sink = jnp.zeros((16, width), F32)
    for head in range(width // HD):
        sink = jnp.where((lane >= head * HD) & (lane < head * HD + HD), sink_ref[head], sink)
    high = sink.astype(BF16).astype(F32)
    middle = (sink - high).astype(BF16).astype(F32)
    low = sink - high - middle
    terms = jnp.where(row == 0, high, jnp.where(row == 1, middle, jnp.where(row == 2, low, 0.0)))
    for number in range(len_ref.shape[1]):
        terms = jnp.where(row == 3 + number, len_ref[0, number].astype(F32), terms)
    for peer in range(PLANE):
        for plane in range(planes):
            block = me ^ (plane * PLANE + peer)
            rows = pl.ds(pl.multiple_of(block * tok_dev, tok_dev), tok_dev)
            turn = block * tok_dev % MAXLEN
            cosine = turn_ref[pl.ds(pl.multiple_of(turn, tok_dev), tok_dev), :]
            sine = turn_ref[pl.ds(pl.multiple_of(turn + MAXLEN, tok_dev), tok_dev), :]
            for pair in range(width // LANES):
                span = slice(pair * LANES, (pair + 1) * LANES)
                query = q_ref[rows, span].astype(F32)
                turned = query * cosine + partner(query) * sine
                out_refs[peer][plane * tok_dev : (plane + 1) * tok_dev, span] = turned.astype(BF16)
        out_refs[peer][planes * tok_dev : planes * tok_dev + 16, :] = terms.astype(BF16)
    step = out_refs[-1].shape[1]
    for number, first in enumerate(range(0, resid_ref.shape[1], step)):
        size = min(step, resid_ref.shape[1] - first)
        rows = slice(number * tok_dev, (number + 1) * tok_dev)
        out_refs[-1][rows, :size] = resid_ref[:, first : first + size]


def rotate_kernel(turn_ref, q_ref, out_ref):
    for req in range(q_ref.shape[0] // MAXLEN):
        rows = slice(req * MAXLEN, (req + 1) * MAXLEN)
        query = q_ref[rows, :].astype(F32)
        turned = query * turn_ref[:MAXLEN] + partner(query) * turn_ref[MAXLEN:]
        out_ref[rows, :] = turned.astype(BF16)


def attend_kernel(blocks, requests, tok_dev, kv_rows, *refs):
    q_refs, kv_ref, w_ref = refs[:blocks], refs[blocks], refs[blocks + 1]
    resid_refs, (out_ref, early_ref, sem) = refs[blocks + 2 : -3], refs[-3:]
    load = pltpu.make_async_copy(w_ref.at[pl.ds(0, early_ref.shape[0])], early_ref, sem)
    load.start()
    rows = q_refs[0].shape[0] - 16
    inner = lax.axis_index("tensor") & (PLANE - 1)
    plane = lax.axis_index("tensor") >> log2(PLANE)
    low = lax.broadcasted_iota(jnp.int32, (kv_ref.shape[0], LANES), 1) < HD

    def doubled(values):
        swapped = pltpu.roll(values, HD, 1)
        return (
            jnp.where(low, values, swapped).astype(BF16),
            jnp.where(low, swapped, values).astype(BF16),
        )

    keys = doubled(kv_ref[:, :LANES].astype(F32))
    vals = doubled(kv_ref[:, LANES:].astype(F32))
    row = lax.broadcasted_iota(jnp.int32, (rows, 1), 0)
    shift = tok_dev.bit_length() - 1
    slot = (((row >> shift) ^ plane) * PLANE + inner) * tok_dev + (row & (tok_dev - 1))
    request = slot >> (MAXLEN.bit_length() - 1)
    length = jnp.zeros_like(slot)
    told = q_refs[0][rows : rows + 16, :LANES].astype(F32)
    for number in range(requests):
        live = told[3 + number : 4 + number, 0:1].astype(jnp.int32)
        length = jnp.where(request == number, live, length)
    base = request * MAXLEN
    last = jnp.minimum(slot, base + length - 1)
    key_row = lax.broadcasted_iota(jnp.int32, (1, kv_ref.shape[0]), 1)
    source = jnp.floor((key_row.astype(F32) + 0.5) * (1.0 / kv_rows)).astype(jnp.int32)
    inside = key_row - source * kv_rows - (kv_rows - tok_dev)
    key_slot = jnp.where(inside < 0, -1, source * tok_dev + inside)
    visible = (key_slot < 0) | ((key_slot >= base) & (key_slot <= last))
    left = lax.broadcasted_iota(jnp.int32, (rows, LANES), 1) < HD
    spans = [slice(pair * LANES, (pair + 1) * LANES) for pair in range(2)]
    if blocks == PLANE:
        sets = [[(block, pair) for block in some for pair in range(2)] for some in ([0], [1], [2], [3])]
    else:
        sets = [[(0, pair)] for pair in range(2)]
    for places in sets:
        half = places[0][0] // 2 if blocks == PLANE else places[0][1]
        stack, sink = [], []
        for block, pair in places:
            query = q_refs[block][:rows, spans[pair]].astype(F32) * 0.125
            stack += [jnp.where(left, query, 0.0), jnp.where(left, 0.0, query)]
            terms = q_refs[block][rows : rows + 16, spans[pair]].astype(F32)
            terms = terms[0:1] + terms[1:2] + terms[2:3]
            sink += [jnp.broadcast_to(terms[:, at : at + 1], (rows, 1)) for at in (0, HD)]
        scores = lax.dot_general(
            jnp.concatenate(stack, axis=0).astype(BF16),
            keys[half],
            (((1,), (1,)), ((), ())),
            preferred_element_type=F32,
        )
        sink = jnp.concatenate(sink, axis=0)
        scores = jnp.where(jnp.concatenate([visible] * len(stack), axis=0), scores, -1e30)
        top = jnp.maximum(jnp.max(scores, axis=1, keepdims=True), sink)
        weights = jnp.exp(scores - top)
        total = jnp.sum(weights, axis=1, keepdims=True) + jnp.exp(sink - top)
        got = jnp.dot(weights.astype(BF16), vals[half], preferred_element_type=F32) / total
        for number, (block, pair) in enumerate(places):
            at = block * 2 * LANES + pair * LANES
            first = 2 * number * rows
            out_ref[:rows, at : at + LANES] = jnp.where(
                left, got[first : first + rows], got[first + rows : first + 2 * rows]
            ).astype(BF16)
    for resid_ref in resid_refs:
        out_ref[rows:, :] = resid_ref[...]
    load.wait()


def project_kernel(tok_dev, groups, att_ref, *refs):
    w_refs, out_refs = refs[: PLANE + 1], refs[PLANE + 1 :]
    depth = w_refs[0].shape[1]
    slots = att_ref.shape[0] // groups
    taken = out_refs[0].shape[0] * len(out_refs) // groups
    rows = jnp.concatenate(
        [att_ref[group * slots : group * slots + taken, :] for group in range(groups)], axis=0
    )

    def times(peer, w_ref):
        return lax.dot_general(
            rows[:, peer * depth : (peer + 1) * depth],
            w_ref[...],
            (((1,), (1,)), ((), ())),
            preferred_element_type=F32,
        )

    far = jnp.concatenate([times(3, w_refs[3]), times(3, w_refs[4])], axis=1)
    whole = times(0, w_refs[0]) + times(1, w_refs[1]) + times(2, w_refs[2]) + far
    slots = taken
    if len(out_refs) == 1:
        out_refs[0][...] = whole
        return
    for plane, out_ref in enumerate(out_refs):
        for group in range(groups):
            first = group * slots + plane * tok_dev
            out_ref[group * tok_dev : (group + 1) * tok_dev, :] = whole[
                first : first + tok_dev
            ].astype(out_ref.dtype)


def split_kernel(top_ref, bottom_ref, top_out, bottom_out, sems):
    first, last = top_out.shape[0], bottom_out.shape[0]
    copies = [
        pltpu.make_async_copy(top_ref.at[pl.ds(0, first)], top_out, sems.at[0]),
        pltpu.make_async_copy(bottom_ref.at[pl.ds(first, last)], bottom_out, sems.at[1]),
    ]
    for copy in copies:
        copy.start()
    for copy in copies:
        copy.wait()


def load_kernel(w_ref, out_ref, sem):
    count = out_ref.shape[0]
    copy = pltpu.make_async_copy(w_ref.at[pl.ds(w_ref.shape[0] - count, count)], out_ref, sem)
    copy.start()
    copy.wait()


def sum_kernel(*refs):
    total = refs[0][...].astype(F32)
    for ref in refs[1:-1]:
        total = total + ref[...].astype(F32)
    refs[-1][...] = total


def dispatch_kernel(
    groups,
    slot_cap,
    tensor_copies,
    pieces_each,
    copies,
    names_ref,
    earlier_ref,
    source_ref,
    gain_ref,
    resid_ref,
    sums_ref,
    resid_out_ref,
    out_ref,
    held,
):
    rows = held.shape[0]
    tok_dev = rows // groups
    width = sums_ref.shape[1]
    for part in range(groups):
        held[:, part * width : (part + 1) * width] = sums_ref[part * rows : (part + 1) * rows, :]
    if resid_ref.shape == held.shape:
        resid = resid_ref[...].astype(F32)
    else:
        each = resid_ref.shape[0] // groups
        step = resid_ref.shape[1]
        count = -(-held.shape[1] // step)
        first = each - count * tok_dev
        resid = jnp.concatenate(
            [
                jnp.concatenate(
                    [
                        resid_ref[
                            group * each + first + number * tok_dev :
                            group * each + first + (number + 1) * tok_dev,
                            : min(step, held.shape[1] - number * step),
                        ].astype(F32)
                        for number in range(count)
                    ],
                    axis=1,
                )
                for group in range(groups)
            ],
            axis=0,
        )
    rounded = (resid + held[...]).astype(BF16)
    wide = rounded.astype(F32)
    own = wide[:tok_dev]
    me_group = lax.axis_index("group")
    for group in range(1, groups):
        own = jnp.where(
            me_group == group, wide[group * tok_dev : (group + 1) * tok_dev], own
        )
    resid_out_ref[...] = own.astype(BF16)
    scale = lax.rsqrt(jnp.mean(wide * wide, axis=1, keepdims=True) + 1e-05)
    normed = (wide * scale * gain_ref[...]).astype(BF16)

    pairs = names_ref.shape[1]
    expert = lax.broadcasted_iota(jnp.int32, (EXPERTS, pairs), 0)
    onehot = (names_ref[...] == expert).astype(F32)
    rank = jnp.dot(onehot.astype(BF16), earlier_ref[...], preferred_element_type=F32)
    pair_rank = jnp.sum(rank * onehot, axis=0, keepdims=True).astype(jnp.int32)
    slot = lax.broadcasted_iota(jnp.int32, (out_ref.shape[0], 1), 0)
    peer = slot >> log2(slot_cap)
    piece = me_group * tensor_copies + (peer & (tensor_copies - 1))
    wanted_rank = (slot & (slot_cap - 1)) * copies + (peer >> log2(tensor_copies))
    picked = (names_ref[...] == piece >> log2(pieces_each)) & (pair_rank == wanted_rank)
    chosen = jnp.dot(picked.astype(F32).astype(BF16), source_ref[...], preferred_element_type=F32)
    out_ref[...] = jnp.dot(chosen.astype(BF16), normed, preferred_element_type=F32).astype(BF16)


def expert_kernel(rows_ref, early_ref, late_ref, out_ref):
    start = early_ref.shape[0]
    width = out_ref.shape[1]
    total = jnp.dot(rows_ref[:, :start], early_ref[...], preferred_element_type=F32)
    total = total + jnp.dot(rows_ref[:, start:], late_ref[...], preferred_element_type=F32)
    gate = jnp.minimum(total[:, :width], 7.0)
    up = jnp.clip(total[:, width : 2 * width], -7.0, 7.0)
    out_ref[...] = ((up + 1.0) * gate / (1.0 + jnp.exp(-1.702 * gate))).astype(BF16)


def local(
    resid_in,
    queries,
    suffix_kv,
    prefix_kv,
    block_map,
    lengths,
    sinks,
    w_out,
    mlp_gain,
    routes,
    w_experts,
):
    groups = lax.axis_size("group")
    tensors = lax.axis_size("tensor")
    me_group = lax.axis_index("group")
    me_tensor = lax.axis_index("tensor")
    block_rows = prefix_kv.shape[1]
    prefix_len = block_rows * tensors
    slot_count = queries.shape[1]
    heads_here = queries.shape[2] // HD
    tok_dev = resid_in.shape[1]
    width = resid_in.shape[2]
    planes = tensors // PLANE
    slots_here = planes * tok_dev
    aligned = tok_dev % 16 == 0 and heads_here % 2 == 0

    def swap(values, bits):
        return lax.ppermute(values, "tensor", [(i, i ^ bits) for i in range(tensors)])

    columns_here = width // groups
    cut = columns_here // 2
    held = lax.dynamic_slice_in_dim(w_out.T, me_group * columns_here, columns_here, 0)
    beside, across = swap(held, 1), swap(held, 2)

    kv_rows = block_rows + tok_dev
    rope = rope_rows()
    angle = (prefix_len + np.arange(MAXLEN)).astype(np.float32)[:, None] * rope[0][None, :]
    turns = np.concatenate([np.cos(angle), np.sin(angle) * rope[1][None, :]], axis=0)
    turns = jnp.asarray(turns.astype(np.float32))
    query_cols = heads_here * HD
    top_count = routes.shape[2]
    pair_count = tok_dev * groups * top_count

    owned = call(
        functools.partial(keys_kernel, heads_here, tensors),
        jax.ShapeDtypeStruct((tensors, kv_rows, 2 * LANES), BF16),
        [SMEM, ANY, ANY],
        "rotate_keys",
        scratch=[
            pltpu.VMEM(suffix_kv.shape[1:], BF16),
            pltpu.VMEM(prefix_kv.shape[1:], BF16),
            pltpu.SemaphoreType.DMA((2,)),
        ],
        limit=60.5,
    )(block_map, suffix_kv[0], prefix_kv[0])
    if aligned:
        extra = -(-width // (PLANE * query_cols)) * tok_dev
        *sent, packed = call(
            functools.partial(queries_kernel, tok_dev),
            [jax.ShapeDtypeStruct((slots_here + 16, query_cols), BF16)] * PLANE
            + [jax.ShapeDtypeStruct((extra, PLANE * query_cols), BF16)],
            [SMEM, SMEM, VMEM, VMEM, VMEM],
            "rotate_queries",
        )(lengths, sinks, turns, queries[0], resid_in[0])
        packed = [packed]
    else:
        extra, packed = 0, []
        padded = jnp.pad(queries[0], ((0, 0), (0, LANES - query_cols)))
        turned = call(
            rotate_kernel,
            jax.ShapeDtypeStruct(padded.shape, BF16),
            [VMEM, VMEM],
            "rotate_queries",
        )(turns, padded)[:, :query_cols]
        turned = turned.reshape(tensors, tok_dev, query_cols)
        turned = jnp.take(turned, me_tensor ^ jnp.arange(tensors), axis=0)
        turned = turned.reshape(planes, PLANE, tok_dev, query_cols)
        spread = jnp.repeat(sinks, HD)
        high = lax.reduce_precision(spread, 8, 7)
        middle = lax.reduce_precision(spread - high, 8, 7)
        told = jnp.broadcast_to(lengths[0].astype(F32)[:, None], (lengths.shape[1], query_cols))
        terms = jnp.concatenate([jnp.stack([high, middle, spread - high - middle]), told], axis=0)
        terms = jnp.pad(terms, ((0, 16 - terms.shape[0]), (0, 0))).astype(BF16)
        sent = [
            jnp.concatenate([turned[:, peer].reshape(slots_here, query_cols), terms], axis=0)
            for peer in range(PLANE)
        ]
    kv = lax.all_to_all(owned, "tensor", split_axis=0, concat_axis=0, tiled=True)
    received = [sent[0]] + [swap(sent[peer], peer) for peer in range(1, PLANE)]
    names, gain = routes.reshape(1, pair_count), mlp_gain[None, :]
    beside, across, names, gain = lax.optimization_barrier((beside, across, names, gain))
    halves = call(
        split_kernel,
        [
            jax.ShapeDtypeStruct((cut, held.shape[1]), BF16),
            jax.ShapeDtypeStruct((columns_here - cut, held.shape[1]), BF16),
        ],
        [ANY, ANY],
        "split",
        scratch=[pltpu.SemaphoreType.DMA((2,))],
        limit=2,
        space=ANY,
    )(beside, across)
    far = [swap(halves[0], 2), swap(halves[1], 1)]
    projections = [held, beside, across, *far]
    kv = kv.reshape(tensors * kv_rows, 2 * LANES)
    if not aligned:
        received = [jnp.concatenate(received, axis=1)]

    columns = w_experts.shape[2]
    early_rows = min(width // 2, 768)
    attended, early = call(
        functools.partial(attend_kernel, len(received), lengths.shape[1], tok_dev, kv_rows),
        [
            jax.ShapeDtypeStruct((slots_here + extra, PLANE * query_cols), BF16),
            jax.ShapeDtypeStruct((early_rows, columns), BF16),
        ],
        [VMEM] * (1 + len(received)) + [ANY] + [VMEM] * len(packed),
        "attend",
        scratch=[pltpu.SemaphoreType.DMA],
        limit=26,
        flops=5000000000,
    )(*received, kv, w_experts[0], *packed)

    attended = lax.all_gather(attended, "group", axis=0, tiled=True)
    rows_here = groups * tok_dev
    if aligned:
        outs = [
            jax.ShapeDtypeStruct((rows_here, columns_here), F32 if plane == 0 else BF16)
            for plane in range(planes)
        ]
    else:
        outs = [jax.ShapeDtypeStruct((groups * slots_here, columns_here), F32)]
    parts = call(
        functools.partial(project_kernel, tok_dev, groups),
        outs,
        [VMEM] * (2 + PLANE),
        "project",
    )(attended, *projections)
    if not aligned:
        split = parts[0].reshape(groups, planes, tok_dev, columns_here)
        parts = [split[:, plane].reshape(rows_here, columns_here) for plane in range(planes)]
        parts = [parts[0]] + [part.astype(BF16) for part in parts[1:]]
    pair_ids = np.arange(pair_count)
    pair_row = pair_ids // top_count % groups * tok_dev + pair_ids // (groups * top_count)
    source = (pair_row[:, None] == np.arange(groups * tok_dev)[None, :]).astype(np.float32)
    earlier = (pair_ids[:, None] < pair_ids[None, :]).astype(np.float32)
    pieces_total = groups * tensors
    pieces_each = min(8, pieces_total // EXPERTS)
    copies = pieces_total // (EXPERTS * pieces_each)
    tensor_copies = tensors // copies
    slot_cap = pair_count // 16 // copies
    resid_all = attended if aligned else lax.all_gather(resid_in[0], "group", axis=0, tiled=True)
    *parts, piece = lax.optimization_barrier((*parts, w_experts[0]))
    arrived = [swap(parts[plane], plane * PLANE) for plane in reversed(range(1, planes))]
    arrived = [parts[0]] + arrived
    late = call(
        load_kernel,
        jax.ShapeDtypeStruct((width - early_rows, columns), BF16),
        [ANY],
        "load_expert",
        scratch=[pltpu.SemaphoreType.DMA],
        limit=4,
        moved=2 * (width - early_rows) * columns * 2,
    )(piece)
    *arrived, late = lax.optimization_barrier((*arrived, late))
    sums = call(
        sum_kernel,
        jax.ShapeDtypeStruct((rows_here, columns_here), F32),
        [VMEM] * planes,
        "sum_planes",
    )(*arrived)
    sums = lax.all_gather(sums, "group", axis=0, tiled=True)

    resid_out, outgoing = call(
        functools.partial(
            dispatch_kernel, groups, slot_cap, tensor_copies, pieces_each, copies
        ),
        [
            jax.ShapeDtypeStruct((tok_dev, width), BF16),
            jax.ShapeDtypeStruct((tensors * slot_cap, width), BF16),
        ],
        [VMEM] * 6,
        "norm_dispatch",
        scratch=[pltpu.VMEM((rows_here, width), F32)],
    )(
        names,
        jnp.asarray(earlier, BF16),
        jnp.asarray(source, BF16),
        gain,
        resid_all,
        sums,
    )
    rows = lax.all_to_all(
        outgoing.reshape(tensors, slot_cap, width),
        "tensor",
        split_axis=0,
        concat_axis=0,
        tiled=True,
    )
    hidden = call(
        expert_kernel,
        jax.ShapeDtypeStruct((tensors * slot_cap, columns // 2), BF16),
        [VMEM] * 3,
        "experts",
        limit=16,
    )(rows.reshape(tensors * slot_cap, width), early, late)
    return (resid_out[None], hidden.reshape(1, tensors, slot_cap, columns // 2))


def solution(mesh):
    placed = (
        P("group", "tensor", None),
        P("group", None, "tensor"),
        P("group", "tensor", None),
        P("group", "tensor", None),
        P("group", "tensor"),
        P("group", None),
        P("tensor"),
        P("tensor", None),
        P(),
        P("tensor", None, None),
        P(("group", "tensor"), None, None),
    )
    return jax.shard_map(
        local,
        mesh=mesh,
        in_specs=placed,
        out_specs=(P("group", "tensor", None), P(("group", "tensor"), None, None, None)),
        check_vma=False,
    )
```

```python
import functools
import math

import jax
import jax.numpy as jnp
import numpy as np
from jax import lax
from jax.experimental import pallas as pl
from jax.experimental.pallas import tpu as pltpu
from jax.sharding import PartitionSpec as P

HEADS = 64
KVH = 8
HD = 64
EXPERTS = 32
MAXLEN = 128
LANES = 128
F32 = jnp.float32
BF16 = jnp.bfloat16
VMEM = pl.BlockSpec(memory_space=pltpu.VMEM)
SMEM = pl.BlockSpec(memory_space=pltpu.SMEM)
ANY = pl.BlockSpec(memory_space=pl.ANY)
PLANE = 4


def call(kernel, outs, specs, name, scratch=(), limit=12, moved=0, space=VMEM, flops=0):
    single = not isinstance(outs, (list, tuple))
    return pl.pallas_call(
        kernel,
        out_shape=outs,
        in_specs=list(specs),
        out_specs=space if single else [space] * len(outs),
        scratch_shapes=list(scratch),
        name=name,
        compiler_params=pltpu.CompilerParams(vmem_limit_bytes=int(limit * 1024 * 1024)),
        cost_estimate=pl.CostEstimate(flops=flops, bytes_accessed=moved, transcendentals=0),
    )


def log2(number):
    assert number & (number - 1) == 0
    return number.bit_length() - 1


def rope_rows():
    lane = np.arange(LANES) % HD
    frequency = np.power(np.float32(150000.0), -2.0 * (lane % (HD // 2)) / HD).astype(np.float32)
    sign = np.where(lane < HD // 2, -1.0, 1.0).astype(np.float32)
    return np.stack([frequency, sign])


def partner(values):
    lane = lax.broadcasted_iota(jnp.int32, values.shape, 1)
    ahead = pltpu.roll(values, LANES - HD // 2, 1)
    behind = pltpu.roll(values, HD // 2, 1)
    return jnp.where(lane % HD < HD // 2, ahead, behind)


def keys_kernel(
    heads_here, tensors, block_ref, suffix_hbm, prefix_hbm, out_ref, suffix_ref, prefix_ref, sems
):
    copies = [
        pltpu.make_async_copy(prefix_hbm, prefix_ref, sems.at[0]),
        pltpu.make_async_copy(suffix_hbm, suffix_ref, sems.at[1]),
    ]
    for copy in copies:
        copy.start()
    block_rows = prefix_ref.shape[0]
    tok_dev = suffix_ref.shape[0]
    prefix_len = block_rows * tensors
    half = KVH * HD
    share = HEADS // KVH

    def part(ref, first, low):
        rows = ref.shape[0]
        row = lax.broadcasted_iota(jnp.int32, (rows, LANES), 0) + first
        lane = lax.broadcasted_iota(jnp.int32, (1, LANES), 1) & (HD - 1)
        exponent = (lane & (HD // 2 - 1)).astype(F32) * (-2.0 * math.log(150000.0) / HD)
        angle = row.astype(F32) * jnp.exp(exponent)
        cosine = jnp.cos(angle)
        sine = jnp.sin(angle) * jnp.where(lane < HD // 2, -1.0, 1.0)
        left = lax.broadcasted_iota(jnp.int32, (rows, LANES), 1) < HD
        made = {}
        for peer in range(tensors):
            one = peer * heads_here // share
            two = (peer ^ 2) * heads_here // share
            if (one, two) not in made:
                pair = one // 2
                keys = ref[:, pair * LANES : (pair + 1) * LANES].astype(F32)
                vals = ref[:, half + pair * LANES : half + (pair + 1) * LANES].astype(F32)
                turned = keys * cosine + partner(keys) * sine

                def ordered(values):
                    swapped = pltpu.roll(values, HD, 1)
                    first_half = values if one % 2 == 0 else swapped
                    second_half = values if two % 2 == 1 else swapped
                    return jnp.where(left, first_half, second_half).astype(BF16)

                made[one, two] = ordered(turned), ordered(vals)
            out_ref[peer, low : low + rows, :LANES] = made[one, two][0]
            out_ref[peer, low : low + rows, LANES:] = made[one, two][1]

    copies[0].wait()
    part(prefix_ref, block_ref[0, 0] * block_rows, 0)
    copies[1].wait()
    part(suffix_ref, prefix_len + lax.axis_index("tensor") * tok_dev % MAXLEN, block_rows)


def queries_kernel(tok_dev, len_ref, sink_ref, turn_ref, q_ref, resid_ref, *out_refs):
    me = lax.axis_index("tensor")
    planes = q_ref.shape[0] // tok_dev // PLANE
    width = q_ref.shape[1]
    lane = lax.broadcasted_iota(jnp.int32, (16, width), 1)
    row = lax.broadcasted_iota(jnp.int32, (16, width), 0)
    sink = jnp.zeros((16, width), F32)
    for head in range(width // HD):
        sink = jnp.where((lane >= head * HD) & (lane < head * HD + HD), sink_ref[head], sink)
    high = sink.astype(BF16).astype(F32)
    middle = (sink - high).astype(BF16).astype(F32)
    low = sink - high - middle
    terms = jnp.where(row == 0, high, jnp.where(row == 1, middle, jnp.where(row == 2, low, 0.0)))
    for number in range(len_ref.shape[1]):
        terms = jnp.where(row == 3 + number, len_ref[0, number].astype(F32), terms)
    for peer in range(PLANE):
        for plane in range(planes):
            block = me ^ (plane * PLANE + peer)
            rows = pl.ds(pl.multiple_of(block * tok_dev, tok_dev), tok_dev)
            turn = block * tok_dev % MAXLEN
            cosine = turn_ref[pl.ds(pl.multiple_of(turn, tok_dev), tok_dev), :]
            sine = turn_ref[pl.ds(pl.multiple_of(turn + MAXLEN, tok_dev), tok_dev), :]
            for pair in range(width // LANES):
                span = slice(pair * LANES, (pair + 1) * LANES)
                query = q_ref[rows, span].astype(F32)
                turned = query * cosine + partner(query) * sine
                out_refs[peer][plane * tok_dev : (plane + 1) * tok_dev, span] = turned.astype(BF16)
        out_refs[peer][planes * tok_dev : planes * tok_dev + 16, :] = terms.astype(BF16)
    step = out_refs[-1].shape[1]
    for number, first in enumerate(range(0, resid_ref.shape[1], step)):
        size = min(step, resid_ref.shape[1] - first)
        rows = slice(number * tok_dev, (number + 1) * tok_dev)
        out_refs[-1][rows, :size] = resid_ref[:, first : first + size]


def rotate_kernel(turn_ref, q_ref, out_ref):
    for req in range(q_ref.shape[0] // MAXLEN):
        rows = slice(req * MAXLEN, (req + 1) * MAXLEN)
        query = q_ref[rows, :].astype(F32)
        turned = query * turn_ref[:MAXLEN] + partner(query) * turn_ref[MAXLEN:]
        out_ref[rows, :] = turned.astype(BF16)


def attend_kernel(blocks, requests, tok_dev, kv_rows, *refs):
    q_refs, kv_ref, w_ref = refs[:blocks], refs[blocks], refs[blocks + 1]
    resid_refs, (out_ref, early_ref, sem) = refs[blocks + 2 : -3], refs[-3:]
    load = pltpu.make_async_copy(w_ref.at[pl.ds(0, early_ref.shape[0])], early_ref, sem)
    load.start()
    rows = q_refs[0].shape[0] - 16
    inner = lax.axis_index("tensor") & (PLANE - 1)
    plane = lax.axis_index("tensor") >> log2(PLANE)
    low = lax.broadcasted_iota(jnp.int32, (kv_ref.shape[0], LANES), 1) < HD

    def doubled(values):
        swapped = pltpu.roll(values, HD, 1)
        return (
            jnp.where(low, values, swapped).astype(BF16),
            jnp.where(low, swapped, values).astype(BF16),
        )

    keys = doubled(kv_ref[:, :LANES].astype(F32))
    vals = doubled(kv_ref[:, LANES:].astype(F32))
    row = lax.broadcasted_iota(jnp.int32, (rows, 1), 0)
    shift = tok_dev.bit_length() - 1
    slot = (((row >> shift) ^ plane) * PLANE + inner) * tok_dev + (row & (tok_dev - 1))
    request = slot >> (MAXLEN.bit_length() - 1)
    length = jnp.zeros_like(slot)
    told = q_refs[0][rows : rows + 16, :LANES].astype(F32)
    for number in range(requests):
        live = told[3 + number : 4 + number, 0:1].astype(jnp.int32)
        length = jnp.where(request == number, live, length)
    base = request * MAXLEN
    last = jnp.minimum(slot, base + length - 1)
    key_row = lax.broadcasted_iota(jnp.int32, (1, kv_ref.shape[0]), 1)
    source = jnp.floor((key_row.astype(F32) + 0.5) * (1.0 / kv_rows)).astype(jnp.int32)
    inside = key_row - source * kv_rows - (kv_rows - tok_dev)
    key_slot = jnp.where(inside < 0, -1, source * tok_dev + inside)
    visible = (key_slot < 0) | ((key_slot >= base) & (key_slot <= last))
    left = lax.broadcasted_iota(jnp.int32, (rows, LANES), 1) < HD
    spans = [slice(pair * LANES, (pair + 1) * LANES) for pair in range(2)]
    if blocks == PLANE:
        sets = [[(block, pair) for block in some for pair in range(2)] for some in ([0], [1], [2], [3])]
    else:
        sets = [[(0, pair)] for pair in range(2)]
    for places in sets:
        half = places[0][0] // 2 if blocks == PLANE else places[0][1]
        stack, sink = [], []
        for block, pair in places:
            query = q_refs[block][:rows, spans[pair]].astype(F32) * 0.125
            stack += [jnp.where(left, query, 0.0), jnp.where(left, 0.0, query)]
            terms = q_refs[block][rows : rows + 16, spans[pair]].astype(F32)
            terms = terms[0:1] + terms[1:2] + terms[2:3]
            sink += [jnp.broadcast_to(terms[:, at : at + 1], (rows, 1)) for at in (0, HD)]
        scores = lax.dot_general(
            jnp.concatenate(stack, axis=0).astype(BF16),
            keys[half],
            (((1,), (1,)), ((), ())),
            preferred_element_type=F32,
        )
        sink = jnp.concatenate(sink, axis=0)
        scores = jnp.where(jnp.concatenate([visible] * len(stack), axis=0), scores, -1e30)
        top = jnp.maximum(jnp.max(scores, axis=1, keepdims=True), sink)
        weights = jnp.exp(scores - top)
        total = jnp.sum(weights, axis=1, keepdims=True) + jnp.exp(sink - top)
        got = jnp.dot(weights.astype(BF16), vals[half], preferred_element_type=F32) / total
        for number, (block, pair) in enumerate(places):
            at = block * 2 * LANES + pair * LANES
            first = 2 * number * rows
            out_ref[:rows, at : at + LANES] = jnp.where(
                left, got[first : first + rows], got[first + rows : first + 2 * rows]
            ).astype(BF16)
    for resid_ref in resid_refs:
        out_ref[rows:, :] = resid_ref[...]
    load.wait()


def project_kernel(tok_dev, groups, att_ref, *refs):
    w_refs, out_refs = refs[: PLANE + 1], refs[PLANE + 1 :]
    depth = w_refs[0].shape[1]
    slots = att_ref.shape[0] // groups
    taken = out_refs[0].shape[0] * len(out_refs) // groups
    rows = jnp.concatenate(
        [att_ref[group * slots : group * slots + taken, :] for group in range(groups)], axis=0
    )

    def times(peer, w_ref):
        return lax.dot_general(
            rows[:, peer * depth : (peer + 1) * depth],
            w_ref[...],
            (((1,), (1,)), ((), ())),
            preferred_element_type=F32,
        )

    far = jnp.concatenate([times(3, w_refs[3]), times(3, w_refs[4])], axis=1)
    whole = times(0, w_refs[0]) + times(1, w_refs[1]) + times(2, w_refs[2]) + far
    slots = taken
    if len(out_refs) == 1:
        out_refs[0][...] = whole
        return
    for plane, out_ref in enumerate(out_refs):
        for group in range(groups):
            first = group * slots + plane * tok_dev
            out_ref[group * tok_dev : (group + 1) * tok_dev, :] = whole[
                first : first + tok_dev
            ].astype(out_ref.dtype)


def split_kernel(top_ref, bottom_ref, top_out, bottom_out, sems):
    first, last = top_out.shape[0], bottom_out.shape[0]
    copies = [
        pltpu.make_async_copy(top_ref.at[pl.ds(0, first)], top_out, sems.at[0]),
        pltpu.make_async_copy(bottom_ref.at[pl.ds(first, last)], bottom_out, sems.at[1]),
    ]
    for copy in copies:
        copy.start()
    for copy in copies:
        copy.wait()


def load_kernel(w_ref, out_ref, sem):
    count = out_ref.shape[0]
    copy = pltpu.make_async_copy(w_ref.at[pl.ds(w_ref.shape[0] - count, count)], out_ref, sem)
    copy.start()
    copy.wait()


def sum_kernel(*refs):
    total = refs[0][...].astype(F32)
    for ref in refs[1:-1]:
        total = total + ref[...].astype(F32)
    refs[-1][...] = total


def dispatch_kernel(
    groups,
    slot_cap,
    tensor_copies,
    pieces_each,
    copies,
    names_ref,
    earlier_ref,
    source_ref,
    gain_ref,
    resid_ref,
    sums_ref,
    resid_out_ref,
    out_ref,
    held,
):
    rows = held.shape[0]
    tok_dev = rows // groups
    width = sums_ref.shape[1]
    for part in range(groups):
        held[:, part * width : (part + 1) * width] = sums_ref[part * rows : (part + 1) * rows, :]
    if resid_ref.shape == held.shape:
        resid = resid_ref[...].astype(F32)
    else:
        each = resid_ref.shape[0] // groups
        step = resid_ref.shape[1]
        count = -(-held.shape[1] // step)
        first = each - count * tok_dev
        resid = jnp.concatenate(
            [
                jnp.concatenate(
                    [
                        resid_ref[
                            group * each + first + number * tok_dev :
                            group * each + first + (number + 1) * tok_dev,
                            : min(step, held.shape[1] - number * step),
                        ].astype(F32)
                        for number in range(count)
                    ],
                    axis=1,
                )
                for group in range(groups)
            ],
            axis=0,
        )
    rounded = (resid + held[...]).astype(BF16)
    wide = rounded.astype(F32)
    own = wide[:tok_dev]
    me_group = lax.axis_index("group")
    for group in range(1, groups):
        own = jnp.where(
            me_group == group, wide[group * tok_dev : (group + 1) * tok_dev], own
        )
    resid_out_ref[...] = own.astype(BF16)
    scale = lax.rsqrt(jnp.mean(wide * wide, axis=1, keepdims=True) + 1e-05)
    normed = (wide * scale * gain_ref[...]).astype(BF16)

    pairs = names_ref.shape[1]
    expert = lax.broadcasted_iota(jnp.int32, (EXPERTS, pairs), 0)
    onehot = (names_ref[...] == expert).astype(F32)
    rank = jnp.dot(onehot.astype(BF16), earlier_ref[...], preferred_element_type=F32)
    pair_rank = jnp.sum(rank * onehot, axis=0, keepdims=True).astype(jnp.int32)
    slot = lax.broadcasted_iota(jnp.int32, (out_ref.shape[0], 1), 0)
    peer = slot >> log2(slot_cap)
    piece = me_group * tensor_copies + (peer & (tensor_copies - 1))
    wanted_rank = (slot & (slot_cap - 1)) * copies + (peer >> log2(tensor_copies))
    picked = (names_ref[...] == piece >> log2(pieces_each)) & (pair_rank == wanted_rank)
    chosen = jnp.dot(picked.astype(F32).astype(BF16), source_ref[...], preferred_element_type=F32)
    out_ref[...] = jnp.dot(chosen.astype(BF16), normed, preferred_element_type=F32).astype(BF16)


def expert_kernel(rows_ref, early_ref, late_ref, out_ref):
    start = early_ref.shape[0]
    width = out_ref.shape[1]
    total = jnp.dot(rows_ref[:, :start], early_ref[...], preferred_element_type=F32)
    total = total + jnp.dot(rows_ref[:, start:], late_ref[...], preferred_element_type=F32)
    gate = jnp.minimum(total[:, :width], 7.0)
    up = jnp.clip(total[:, width : 2 * width], -7.0, 7.0)
    out_ref[...] = ((up + 1.0) * gate / (1.0 + jnp.exp(-1.702 * gate))).astype(BF16)


def local(
    resid_in,
    queries,
    suffix_kv,
    prefix_kv,
    block_map,
    lengths,
    sinks,
    w_out,
    mlp_gain,
    routes,
    w_experts,
):
    groups = lax.axis_size("group")
    tensors = lax.axis_size("tensor")
    me_group = lax.axis_index("group")
    me_tensor = lax.axis_index("tensor")
    block_rows = prefix_kv.shape[1]
    prefix_len = block_rows * tensors
    slot_count = queries.shape[1]
    heads_here = queries.shape[2] // HD
    tok_dev = resid_in.shape[1]
    width = resid_in.shape[2]
    planes = tensors // PLANE
    slots_here = planes * tok_dev
    aligned = tok_dev % 16 == 0 and heads_here % 2 == 0

    def swap(values, bits):
        return lax.ppermute(values, "tensor", [(i, i ^ bits) for i in range(tensors)])

    columns_here = width // groups
    cut = columns_here // 2
    held = lax.dynamic_slice_in_dim(w_out.T, me_group * columns_here, columns_here, 0)
    beside, across = swap(held, 1), swap(held, 2)

    kv_rows = block_rows + tok_dev
    rope = rope_rows()
    angle = (prefix_len + np.arange(MAXLEN)).astype(np.float32)[:, None] * rope[0][None, :]
    turns = np.concatenate([np.cos(angle), np.sin(angle) * rope[1][None, :]], axis=0)
    turns = jnp.asarray(turns.astype(np.float32))
    query_cols = heads_here * HD
    top_count = routes.shape[2]
    pair_count = tok_dev * groups * top_count

    owned = call(
        functools.partial(keys_kernel, heads_here, tensors),
        jax.ShapeDtypeStruct((tensors, kv_rows, 2 * LANES), BF16),
        [SMEM, ANY, ANY],
        "rotate_keys",
        scratch=[
            pltpu.VMEM(suffix_kv.shape[1:], BF16),
            pltpu.VMEM(prefix_kv.shape[1:], BF16),
            pltpu.SemaphoreType.DMA((2,)),
        ],
        limit=60.5,
    )(block_map, suffix_kv[0], prefix_kv[0])
    if aligned:
        extra = -(-width // (PLANE * query_cols)) * tok_dev
        *sent, packed = call(
            functools.partial(queries_kernel, tok_dev),
            [jax.ShapeDtypeStruct((slots_here + 16, query_cols), BF16)] * PLANE
            + [jax.ShapeDtypeStruct((extra, PLANE * query_cols), BF16)],
            [SMEM, SMEM, VMEM, VMEM, VMEM],
            "rotate_queries",
        )(lengths, sinks, turns, queries[0], resid_in[0])
        packed = [packed]
    else:
        extra, packed = 0, []
        padded = jnp.pad(queries[0], ((0, 0), (0, LANES - query_cols)))
        turned = call(
            rotate_kernel,
            jax.ShapeDtypeStruct(padded.shape, BF16),
            [VMEM, VMEM],
            "rotate_queries",
        )(turns, padded)[:, :query_cols]
        turned = turned.reshape(tensors, tok_dev, query_cols)
        turned = jnp.take(turned, me_tensor ^ jnp.arange(tensors), axis=0)
        turned = turned.reshape(planes, PLANE, tok_dev, query_cols)
        spread = jnp.repeat(sinks, HD)
        high = lax.reduce_precision(spread, 8, 7)
        middle = lax.reduce_precision(spread - high, 8, 7)
        told = jnp.broadcast_to(lengths[0].astype(F32)[:, None], (lengths.shape[1], query_cols))
        terms = jnp.concatenate([jnp.stack([high, middle, spread - high - middle]), told], axis=0)
        terms = jnp.pad(terms, ((0, 16 - terms.shape[0]), (0, 0))).astype(BF16)
        sent = [
            jnp.concatenate([turned[:, peer].reshape(slots_here, query_cols), terms], axis=0)
            for peer in range(PLANE)
        ]
    kv = lax.all_to_all(owned, "tensor", split_axis=0, concat_axis=0, tiled=True)
    received = [sent[0]] + [swap(sent[peer], peer) for peer in range(1, PLANE)]
    names, gain = routes.reshape(1, pair_count), mlp_gain[None, :]
    beside, across, names, gain = lax.optimization_barrier((beside, across, names, gain))
    halves = call(
        split_kernel,
        [
            jax.ShapeDtypeStruct((cut, held.shape[1]), BF16),
            jax.ShapeDtypeStruct((columns_here - cut, held.shape[1]), BF16),
        ],
        [ANY, ANY],
        "split",
        scratch=[pltpu.SemaphoreType.DMA((2,))],
        limit=2,
        space=ANY,
    )(beside, across)
    far = [swap(halves[0], 2), swap(halves[1], 1)]
    projections = [held, beside, across, *far]
    kv = kv.reshape(tensors * kv_rows, 2 * LANES)
    if not aligned:
        received = [jnp.concatenate(received, axis=1)]

    columns = w_experts.shape[2]
    early_rows = min(width // 2, 1024)
    attended, early = call(
        functools.partial(attend_kernel, len(received), lengths.shape[1], tok_dev, kv_rows),
        [
            jax.ShapeDtypeStruct((slots_here + extra, PLANE * query_cols), BF16),
            jax.ShapeDtypeStruct((early_rows, columns), BF16),
        ],
        [VMEM] * (1 + len(received)) + [ANY] + [VMEM] * len(packed),
        "attend",
        scratch=[pltpu.SemaphoreType.DMA],
        limit=26,
        flops=5000000000,
    )(*received, kv, w_experts[0], *packed)

    attended = lax.all_gather(attended, "group", axis=0, tiled=True)
    rows_here = groups * tok_dev
    if aligned:
        outs = [
            jax.ShapeDtypeStruct((rows_here, columns_here), F32 if plane == 0 else BF16)
            for plane in range(planes)
        ]
    else:
        outs = [jax.ShapeDtypeStruct((groups * slots_here, columns_here), F32)]
    parts = call(
        functools.partial(project_kernel, tok_dev, groups),
        outs,
        [VMEM] * (2 + PLANE),
        "project",
    )(attended, *projections)
    if not aligned:
        split = parts[0].reshape(groups, planes, tok_dev, columns_here)
        parts = [split[:, plane].reshape(rows_here, columns_here) for plane in range(planes)]
        parts = [parts[0]] + [part.astype(BF16) for part in parts[1:]]
    pair_ids = np.arange(pair_count)
    pair_row = pair_ids // top_count % groups * tok_dev + pair_ids // (groups * top_count)
    source = (pair_row[:, None] == np.arange(groups * tok_dev)[None, :]).astype(np.float32)
    earlier = (pair_ids[:, None] < pair_ids[None, :]).astype(np.float32)
    pieces_total = groups * tensors
    pieces_each = min(8, pieces_total // EXPERTS)
    copies = pieces_total // (EXPERTS * pieces_each)
    tensor_copies = tensors // copies
    slot_cap = pair_count // 16 // copies
    resid_all = attended if aligned else lax.all_gather(resid_in[0], "group", axis=0, tiled=True)
    *parts, piece = lax.optimization_barrier((*parts, w_experts[0]))
    arrived = [swap(parts[plane], plane * PLANE) for plane in reversed(range(1, planes))]
    arrived = [parts[0]] + arrived
    late = call(
        load_kernel,
        jax.ShapeDtypeStruct((width - early_rows, columns), BF16),
        [ANY],
        "load_expert",
        scratch=[pltpu.SemaphoreType.DMA],
        limit=4,
        moved=2 * (width - early_rows) * columns * 2,
    )(piece)
    *arrived, late = lax.optimization_barrier((*arrived, late))
    sums = call(
        sum_kernel,
        jax.ShapeDtypeStruct((rows_here, columns_here), F32),
        [VMEM] * planes,
        "sum_planes",
    )(*arrived)
    sums = lax.all_gather(sums, "group", axis=0, tiled=True)

    resid_out, outgoing = call(
        functools.partial(
            dispatch_kernel, groups, slot_cap, tensor_copies, pieces_each, copies
        ),
        [
            jax.ShapeDtypeStruct((tok_dev, width), BF16),
            jax.ShapeDtypeStruct((tensors * slot_cap, width), BF16),
        ],
        [VMEM] * 6,
        "norm_dispatch",
        scratch=[pltpu.VMEM((rows_here, width), F32)],
    )(
        names,
        jnp.asarray(earlier, BF16),
        jnp.asarray(source, BF16),
        gain,
        resid_all,
        sums,
    )
    rows = lax.all_to_all(
        outgoing.reshape(tensors, slot_cap, width),
        "tensor",
        split_axis=0,
        concat_axis=0,
        tiled=True,
    )
    hidden = call(
        expert_kernel,
        jax.ShapeDtypeStruct((tensors * slot_cap, columns // 2), BF16),
        [VMEM] * 3,
        "experts",
        limit=16,
    )(rows.reshape(tensors * slot_cap, width), early, late)
    return (resid_out[None], hidden.reshape(1, tensors, slot_cap, columns // 2))


def solution(mesh):
    placed = (
        P("group", "tensor", None),
        P("group", None, "tensor"),
        P("group", "tensor", None),
        P("group", "tensor", None),
        P("group", "tensor"),
        P("group", None),
        P("tensor"),
        P("tensor", None),
        P(),
        P("tensor", None, None),
        P(("group", "tensor"), None, None),
    )
    return jax.shard_map(
        local,
        mesh=mesh,
        in_specs=placed,
        out_specs=(P("group", "tensor", None), P(("group", "tensor"), None, None, None)),
        check_vma=False,
    )
```

```python
import functools
import math

import jax
import jax.numpy as jnp
import numpy as np
from jax import lax
from jax.experimental import pallas as pl
from jax.experimental.pallas import tpu as pltpu
from jax.sharding import PartitionSpec as P

HEADS = 64
KVH = 8
HD = 64
EXPERTS = 32
MAXLEN = 128
LANES = 128
F32 = jnp.float32
BF16 = jnp.bfloat16
VMEM = pl.BlockSpec(memory_space=pltpu.VMEM)
SMEM = pl.BlockSpec(memory_space=pltpu.SMEM)
ANY = pl.BlockSpec(memory_space=pl.ANY)
PLANE = 4


def call(kernel, outs, specs, name, scratch=(), limit=12, moved=0, space=VMEM, flops=0):
    single = not isinstance(outs, (list, tuple))
    return pl.pallas_call(
        kernel,
        out_shape=outs,
        in_specs=list(specs),
        out_specs=space if single else [space] * len(outs),
        scratch_shapes=list(scratch),
        name=name,
        compiler_params=pltpu.CompilerParams(vmem_limit_bytes=int(limit * 1024 * 1024)),
        cost_estimate=pl.CostEstimate(flops=flops, bytes_accessed=moved, transcendentals=0),
    )


def log2(number):
    assert number & (number - 1) == 0
    return number.bit_length() - 1


def rope_rows():
    lane = np.arange(LANES) % HD
    frequency = np.power(np.float32(150000.0), -2.0 * (lane % (HD // 2)) / HD).astype(np.float32)
    sign = np.where(lane < HD // 2, -1.0, 1.0).astype(np.float32)
    return np.stack([frequency, sign])


def partner(values):
    lane = lax.broadcasted_iota(jnp.int32, values.shape, 1)
    ahead = pltpu.roll(values, LANES - HD // 2, 1)
    behind = pltpu.roll(values, HD // 2, 1)
    return jnp.where(lane % HD < HD // 2, ahead, behind)


def keys_kernel(
    heads_here, tensors, block_ref, suffix_hbm, prefix_hbm, out_ref, suffix_ref, prefix_ref, sems
):
    copies = [
        pltpu.make_async_copy(prefix_hbm, prefix_ref, sems.at[0]),
        pltpu.make_async_copy(suffix_hbm, suffix_ref, sems.at[1]),
    ]
    for copy in copies:
        copy.start()
    block_rows = prefix_ref.shape[0]
    tok_dev = suffix_ref.shape[0]
    prefix_len = block_rows * tensors
    half = KVH * HD
    share = HEADS // KVH

    def part(ref, first, low):
        rows = ref.shape[0]
        row = lax.broadcasted_iota(jnp.int32, (rows, LANES), 0) + first
        lane = lax.broadcasted_iota(jnp.int32, (1, LANES), 1) & (HD - 1)
        exponent = (lane & (HD // 2 - 1)).astype(F32) * (-2.0 * math.log(150000.0) / HD)
        angle = row.astype(F32) * jnp.exp(exponent)
        cosine = jnp.cos(angle)
        sine = jnp.sin(angle) * jnp.where(lane < HD // 2, -1.0, 1.0)
        left = lax.broadcasted_iota(jnp.int32, (rows, LANES), 1) < HD
        made = {}
        for peer in range(tensors):
            one = peer * heads_here // share
            two = (peer ^ 2) * heads_here // share
            if (one, two) not in made:
                pair = one // 2
                keys = ref[:, pair * LANES : (pair + 1) * LANES].astype(F32)
                vals = ref[:, half + pair * LANES : half + (pair + 1) * LANES].astype(F32)
                turned = keys * cosine + partner(keys) * sine

                def ordered(values):
                    swapped = pltpu.roll(values, HD, 1)
                    first_half = values if one % 2 == 0 else swapped
                    second_half = values if two % 2 == 1 else swapped
                    return jnp.where(left, first_half, second_half).astype(BF16)

                made[one, two] = ordered(turned), ordered(vals)
            out_ref[peer, low : low + rows, :LANES] = made[one, two][0]
            out_ref[peer, low : low + rows, LANES:] = made[one, two][1]

    copies[0].wait()
    part(prefix_ref, block_ref[0, 0] * block_rows, 0)
    copies[1].wait()
    part(suffix_ref, prefix_len + lax.axis_index("tensor") * tok_dev % MAXLEN, block_rows)


def queries_kernel(tok_dev, len_ref, sink_ref, turn_ref, q_ref, resid_ref, *out_refs):
    me = lax.axis_index("tensor")
    planes = q_ref.shape[0] // tok_dev // PLANE
    width = q_ref.shape[1]
    lane = lax.broadcasted_iota(jnp.int32, (16, width), 1)
    row = lax.broadcasted_iota(jnp.int32, (16, width), 0)
    sink = jnp.zeros((16, width), F32)
    for head in range(width // HD):
        sink = jnp.where((lane >= head * HD) & (lane < head * HD + HD), sink_ref[head], sink)
    high = sink.astype(BF16).astype(F32)
    middle = (sink - high).astype(BF16).astype(F32)
    low = sink - high - middle
    terms = jnp.where(row == 0, high, jnp.where(row == 1, middle, jnp.where(row == 2, low, 0.0)))
    for number in range(len_ref.shape[1]):
        terms = jnp.where(row == 3 + number, len_ref[0, number].astype(F32), terms)
    for peer in range(PLANE):
        for plane in range(planes):
            block = me ^ (plane * PLANE + peer)
            rows = pl.ds(pl.multiple_of(block * tok_dev, tok_dev), tok_dev)
            turn = block * tok_dev % MAXLEN
            cosine = turn_ref[pl.ds(pl.multiple_of(turn, tok_dev), tok_dev), :]
            sine = turn_ref[pl.ds(pl.multiple_of(turn + MAXLEN, tok_dev), tok_dev), :]
            for pair in range(width // LANES):
                span = slice(pair * LANES, (pair + 1) * LANES)
                query = q_ref[rows, span].astype(F32)
                turned = query * cosine + partner(query) * sine
                out_refs[peer][plane * tok_dev : (plane + 1) * tok_dev, span] = turned.astype(BF16)
        out_refs[peer][planes * tok_dev : planes * tok_dev + 16, :] = terms.astype(BF16)
    step = out_refs[-1].shape[1]
    for number, first in enumerate(range(0, resid_ref.shape[1], step)):
        size = min(step, resid_ref.shape[1] - first)
        rows = slice(number * tok_dev, (number + 1) * tok_dev)
        out_refs[-1][rows, :size] = resid_ref[:, first : first + size]


def rotate_kernel(turn_ref, q_ref, out_ref):
    for req in range(q_ref.shape[0] // MAXLEN):
        rows = slice(req * MAXLEN, (req + 1) * MAXLEN)
        query = q_ref[rows, :].astype(F32)
        turned = query * turn_ref[:MAXLEN] + partner(query) * turn_ref[MAXLEN:]
        out_ref[rows, :] = turned.astype(BF16)


def attend_kernel(blocks, requests, tok_dev, kv_rows, *refs):
    q_refs, kv_ref, w_ref = refs[:blocks], refs[blocks], refs[blocks + 1]
    resid_refs, (out_ref, early_ref, sems) = refs[blocks + 2 : -3], refs[-3:]
    share = early_ref.shape[0] // 4
    loads = [
        pltpu.make_async_copy(
            w_ref.at[pl.ds(k * share, share)], early_ref.at[pl.ds(k * share, share)], sems.at[k]
        )
        for k in range(4)
    ]
    for load in loads:
        load.start()
    rows = q_refs[0].shape[0] - 16
    inner = lax.axis_index("tensor") & (PLANE - 1)
    plane = lax.axis_index("tensor") >> log2(PLANE)
    low = lax.broadcasted_iota(jnp.int32, (kv_ref.shape[0], LANES), 1) < HD

    def doubled(values):
        swapped = pltpu.roll(values, HD, 1)
        return (
            jnp.where(low, values, swapped).astype(BF16),
            jnp.where(low, swapped, values).astype(BF16),
        )

    keys = doubled(kv_ref[:, :LANES].astype(F32))
    vals = doubled(kv_ref[:, LANES:].astype(F32))
    row = lax.broadcasted_iota(jnp.int32, (rows, 1), 0)
    shift = tok_dev.bit_length() - 1
    slot = (((row >> shift) ^ plane) * PLANE + inner) * tok_dev + (row & (tok_dev - 1))
    request = slot >> (MAXLEN.bit_length() - 1)
    length = jnp.zeros_like(slot)
    told = q_refs[0][rows : rows + 16, :LANES].astype(F32)
    for number in range(requests):
        live = told[3 + number : 4 + number, 0:1].astype(jnp.int32)
        length = jnp.where(request == number, live, length)
    base = request * MAXLEN
    last = jnp.minimum(slot, base + length - 1)
    key_row = lax.broadcasted_iota(jnp.int32, (1, kv_ref.shape[0]), 1)
    source = jnp.floor((key_row.astype(F32) + 0.5) * (1.0 / kv_rows)).astype(jnp.int32)
    inside = key_row - source * kv_rows - (kv_rows - tok_dev)
    key_slot = jnp.where(inside < 0, -1, source * tok_dev + inside)
    visible = (key_slot < 0) | ((key_slot >= base) & (key_slot <= last))
    left = lax.broadcasted_iota(jnp.int32, (rows, LANES), 1) < HD
    spans = [slice(pair * LANES, (pair + 1) * LANES) for pair in range(2)]
    if blocks == PLANE:
        sets = [[(block, pair) for block in some for pair in range(2)] for some in ([0], [1], [2], [3])]
    else:
        sets = [[(0, pair)] for pair in range(2)]
    for places in sets:
        half = places[0][0] // 2 if blocks == PLANE else places[0][1]
        stack, sink = [], []
        for block, pair in places:
            query = q_refs[block][:rows, spans[pair]].astype(F32) * 0.125
            stack += [jnp.where(left, query, 0.0), jnp.where(left, 0.0, query)]
            terms = q_refs[block][rows : rows + 16, spans[pair]].astype(F32)
            terms = terms[0:1] + terms[1:2] + terms[2:3]
            sink += [jnp.broadcast_to(terms[:, at : at + 1], (rows, 1)) for at in (0, HD)]
        scores = lax.dot_general(
            jnp.concatenate(stack, axis=0).astype(BF16),
            keys[half],
            (((1,), (1,)), ((), ())),
            preferred_element_type=F32,
        )
        sink = jnp.concatenate(sink, axis=0)
        scores = jnp.where(jnp.concatenate([visible] * len(stack), axis=0), scores, -1e30)
        top = jnp.maximum(jnp.max(scores, axis=1, keepdims=True), sink)
        weights = jnp.exp(scores - top)
        total = jnp.sum(weights, axis=1, keepdims=True) + jnp.exp(sink - top)
        got = jnp.dot(weights.astype(BF16), vals[half], preferred_element_type=F32) / total
        for number, (block, pair) in enumerate(places):
            at = block * 2 * LANES + pair * LANES
            first = 2 * number * rows
            out_ref[:rows, at : at + LANES] = jnp.where(
                left, got[first : first + rows], got[first + rows : first + 2 * rows]
            ).astype(BF16)
    for resid_ref in resid_refs:
        out_ref[rows:, :] = resid_ref[...]
    for load in loads:
        load.wait()


def project_kernel(tok_dev, groups, att_ref, *refs):
    w_refs, out_refs = refs[: PLANE + 1], refs[PLANE + 1 :]
    depth = w_refs[0].shape[1]
    slots = att_ref.shape[0] // groups
    taken = out_refs[0].shape[0] * len(out_refs) // groups
    rows = jnp.concatenate(
        [att_ref[group * slots : group * slots + taken, :] for group in range(groups)], axis=0
    )

    def times(peer, w_ref):
        return lax.dot_general(
            rows[:, peer * depth : (peer + 1) * depth],
            w_ref[...],
            (((1,), (1,)), ((), ())),
            preferred_element_type=F32,
        )

    far = jnp.concatenate([times(3, w_refs[3]), times(3, w_refs[4])], axis=1)
    whole = times(0, w_refs[0]) + times(1, w_refs[1]) + times(2, w_refs[2]) + far
    slots = taken
    if len(out_refs) == 1:
        out_refs[0][...] = whole
        return
    for plane, out_ref in enumerate(out_refs):
        for group in range(groups):
            first = group * slots + plane * tok_dev
            out_ref[group * tok_dev : (group + 1) * tok_dev, :] = whole[
                first : first + tok_dev
            ].astype(out_ref.dtype)


def split_kernel(top_ref, bottom_ref, top_out, bottom_out, sems):
    first, last = top_out.shape[0], bottom_out.shape[0]
    copies = [
        pltpu.make_async_copy(top_ref.at[pl.ds(0, first)], top_out, sems.at[0]),
        pltpu.make_async_copy(bottom_ref.at[pl.ds(first, last)], bottom_out, sems.at[1]),
    ]
    for copy in copies:
        copy.start()
    for copy in copies:
        copy.wait()


def load_kernel(w_ref, out_ref, sem):
    count = out_ref.shape[0]
    copy = pltpu.make_async_copy(w_ref.at[pl.ds(w_ref.shape[0] - count, count)], out_ref, sem)
    copy.start()
    copy.wait()


def sum_kernel(*refs):
    total = refs[0][...].astype(F32)
    for ref in refs[1:-1]:
        total = total + ref[...].astype(F32)
    refs[-1][...] = total


def dispatch_kernel(
    groups,
    slot_cap,
    tensor_copies,
    pieces_each,
    copies,
    names_ref,
    earlier_ref,
    source_ref,
    gain_ref,
    resid_ref,
    sums_ref,
    resid_out_ref,
    out_ref,
    held,
):
    rows = held.shape[0]
    tok_dev = rows // groups
    width = sums_ref.shape[1]
    for part in range(groups):
        held[:, part * width : (part + 1) * width] = sums_ref[part * rows : (part + 1) * rows, :]
    if resid_ref.shape == held.shape:
        resid = resid_ref[...].astype(F32)
    else:
        each = resid_ref.shape[0] // groups
        step = resid_ref.shape[1]
        count = -(-held.shape[1] // step)
        first = each - count * tok_dev
        resid = jnp.concatenate(
            [
                jnp.concatenate(
                    [
                        resid_ref[
                            group * each + first + number * tok_dev :
                            group * each + first + (number + 1) * tok_dev,
                            : min(step, held.shape[1] - number * step),
                        ].astype(F32)
                        for number in range(count)
                    ],
                    axis=1,
                )
                for group in range(groups)
            ],
            axis=0,
        )
    rounded = (resid + held[...]).astype(BF16)
    wide = rounded.astype(F32)
    own = wide[:tok_dev]
    me_group = lax.axis_index("group")
    for group in range(1, groups):
        own = jnp.where(
            me_group == group, wide[group * tok_dev : (group + 1) * tok_dev], own
        )
    resid_out_ref[...] = own.astype(BF16)
    scale = lax.rsqrt(jnp.mean(wide * wide, axis=1, keepdims=True) + 1e-05)
    normed = (wide * scale * gain_ref[...]).astype(BF16)

    pairs = names_ref.shape[1]
    expert = lax.broadcasted_iota(jnp.int32, (EXPERTS, pairs), 0)
    onehot = (names_ref[...] == expert).astype(F32)
    rank = jnp.dot(onehot.astype(BF16), earlier_ref[...], preferred_element_type=F32)
    pair_rank = jnp.sum(rank * onehot, axis=0, keepdims=True).astype(jnp.int32)
    slot = lax.broadcasted_iota(jnp.int32, (out_ref.shape[0], 1), 0)
    peer = slot >> log2(slot_cap)
    piece = me_group * tensor_copies + (peer & (tensor_copies - 1))
    wanted_rank = (slot & (slot_cap - 1)) * copies + (peer >> log2(tensor_copies))
    picked = (names_ref[...] == piece >> log2(pieces_each)) & (pair_rank == wanted_rank)
    chosen = jnp.dot(picked.astype(F32).astype(BF16), source_ref[...], preferred_element_type=F32)
    out_ref[...] = jnp.dot(chosen.astype(BF16), normed, preferred_element_type=F32).astype(BF16)


def expert_kernel(rows_ref, early_ref, late_ref, out_ref):
    start = early_ref.shape[0]
    width = out_ref.shape[1]
    total = jnp.dot(rows_ref[:, :start], early_ref[...], preferred_element_type=F32)
    total = total + jnp.dot(rows_ref[:, start:], late_ref[...], preferred_element_type=F32)
    gate = jnp.minimum(total[:, :width], 7.0)
    up = jnp.clip(total[:, width : 2 * width], -7.0, 7.0)
    out_ref[...] = ((up + 1.0) * gate / (1.0 + jnp.exp(-1.702 * gate))).astype(BF16)


def local(
    resid_in,
    queries,
    suffix_kv,
    prefix_kv,
    block_map,
    lengths,
    sinks,
    w_out,
    mlp_gain,
    routes,
    w_experts,
):
    groups = lax.axis_size("group")
    tensors = lax.axis_size("tensor")
    me_group = lax.axis_index("group")
    me_tensor = lax.axis_index("tensor")
    block_rows = prefix_kv.shape[1]
    prefix_len = block_rows * tensors
    slot_count = queries.shape[1]
    heads_here = queries.shape[2] // HD
    tok_dev = resid_in.shape[1]
    width = resid_in.shape[2]
    planes = tensors // PLANE
    slots_here = planes * tok_dev
    aligned = tok_dev % 16 == 0 and heads_here % 2 == 0

    def swap(values, bits):
        return lax.ppermute(values, "tensor", [(i, i ^ bits) for i in range(tensors)])

    columns_here = width // groups
    cut = columns_here // 2
    held = lax.dynamic_slice_in_dim(w_out.T, me_group * columns_here, columns_here, 0)
    beside, across = swap(held, 1), swap(held, 2)

    kv_rows = block_rows + tok_dev
    rope = rope_rows()
    angle = (prefix_len + np.arange(MAXLEN)).astype(np.float32)[:, None] * rope[0][None, :]
    turns = np.concatenate([np.cos(angle), np.sin(angle) * rope[1][None, :]], axis=0)
    turns = jnp.asarray(turns.astype(np.float32))
    query_cols = heads_here * HD
    top_count = routes.shape[2]
    pair_count = tok_dev * groups * top_count

    owned = call(
        functools.partial(keys_kernel, heads_here, tensors),
        jax.ShapeDtypeStruct((tensors, kv_rows, 2 * LANES), BF16),
        [SMEM, ANY, ANY],
        "rotate_keys",
        scratch=[
            pltpu.VMEM(suffix_kv.shape[1:], BF16),
            pltpu.VMEM(prefix_kv.shape[1:], BF16),
            pltpu.SemaphoreType.DMA((2,)),
        ],
        limit=60.5,
    )(block_map, suffix_kv[0], prefix_kv[0])
    if aligned:
        extra = -(-width // (PLANE * query_cols)) * tok_dev
        *sent, packed = call(
            functools.partial(queries_kernel, tok_dev),
            [jax.ShapeDtypeStruct((slots_here + 16, query_cols), BF16)] * PLANE
            + [jax.ShapeDtypeStruct((extra, PLANE * query_cols), BF16)],
            [SMEM, SMEM, VMEM, VMEM, VMEM],
            "rotate_queries",
        )(lengths, sinks, turns, queries[0], resid_in[0])
        packed = [packed]
    else:
        extra, packed = 0, []
        padded = jnp.pad(queries[0], ((0, 0), (0, LANES - query_cols)))
        turned = call(
            rotate_kernel,
            jax.ShapeDtypeStruct(padded.shape, BF16),
            [VMEM, VMEM],
            "rotate_queries",
        )(turns, padded)[:, :query_cols]
        turned = turned.reshape(tensors, tok_dev, query_cols)
        turned = jnp.take(turned, me_tensor ^ jnp.arange(tensors), axis=0)
        turned = turned.reshape(planes, PLANE, tok_dev, query_cols)
        spread = jnp.repeat(sinks, HD)
        high = lax.reduce_precision(spread, 8, 7)
        middle = lax.reduce_precision(spread - high, 8, 7)
        told = jnp.broadcast_to(lengths[0].astype(F32)[:, None], (lengths.shape[1], query_cols))
        terms = jnp.concatenate([jnp.stack([high, middle, spread - high - middle]), told], axis=0)
        terms = jnp.pad(terms, ((0, 16 - terms.shape[0]), (0, 0))).astype(BF16)
        sent = [
            jnp.concatenate([turned[:, peer].reshape(slots_here, query_cols), terms], axis=0)
            for peer in range(PLANE)
        ]
    kv = lax.all_to_all(owned, "tensor", split_axis=0, concat_axis=0, tiled=True)
    received = [sent[0]] + [swap(sent[peer], peer) for peer in range(1, PLANE)]
    names, gain = routes.reshape(1, pair_count), mlp_gain[None, :]
    beside, across, names, gain = lax.optimization_barrier((beside, across, names, gain))
    halves = call(
        split_kernel,
        [
            jax.ShapeDtypeStruct((cut, held.shape[1]), BF16),
            jax.ShapeDtypeStruct((columns_here - cut, held.shape[1]), BF16),
        ],
        [ANY, ANY],
        "split",
        scratch=[pltpu.SemaphoreType.DMA((2,))],
        limit=2,
        space=ANY,
    )(beside, across)
    far = [swap(halves[0], 2), swap(halves[1], 1)]
    projections = [held, beside, across, *far]
    kv = kv.reshape(tensors * kv_rows, 2 * LANES)
    if not aligned:
        received = [jnp.concatenate(received, axis=1)]

    columns = w_experts.shape[2]
    early_rows = min(width // 2, 1024)
    attended, early = call(
        functools.partial(attend_kernel, len(received), lengths.shape[1], tok_dev, kv_rows),
        [
            jax.ShapeDtypeStruct((slots_here + extra, PLANE * query_cols), BF16),
            jax.ShapeDtypeStruct((early_rows, columns), BF16),
        ],
        [VMEM] * (1 + len(received)) + [ANY] + [VMEM] * len(packed),
        "attend",
        scratch=[pltpu.SemaphoreType.DMA((4,))],
        limit=26,
        flops=5000000000,
    )(*received, kv, w_experts[0], *packed)

    attended = lax.all_gather(attended, "group", axis=0, tiled=True)
    rows_here = groups * tok_dev
    if aligned:
        outs = [
            jax.ShapeDtypeStruct((rows_here, columns_here), F32 if plane == 0 else BF16)
            for plane in range(planes)
        ]
    else:
        outs = [jax.ShapeDtypeStruct((groups * slots_here, columns_here), F32)]
    parts = call(
        functools.partial(project_kernel, tok_dev, groups),
        outs,
        [VMEM] * (2 + PLANE),
        "project",
    )(attended, *projections)
    if not aligned:
        split = parts[0].reshape(groups, planes, tok_dev, columns_here)
        parts = [split[:, plane].reshape(rows_here, columns_here) for plane in range(planes)]
        parts = [parts[0]] + [part.astype(BF16) for part in parts[1:]]
    pair_ids = np.arange(pair_count)
    pair_row = pair_ids // top_count % groups * tok_dev + pair_ids // (groups * top_count)
    source = (pair_row[:, None] == np.arange(groups * tok_dev)[None, :]).astype(np.float32)
    earlier = (pair_ids[:, None] < pair_ids[None, :]).astype(np.float32)
    pieces_total = groups * tensors
    pieces_each = min(8, pieces_total // EXPERTS)
    copies = pieces_total // (EXPERTS * pieces_each)
    tensor_copies = tensors // copies
    slot_cap = pair_count // 16 // copies
    resid_all = attended if aligned else lax.all_gather(resid_in[0], "group", axis=0, tiled=True)
    *parts, piece = lax.optimization_barrier((*parts, w_experts[0]))
    arrived = [swap(parts[plane], plane * PLANE) for plane in reversed(range(1, planes))]
    arrived = [parts[0]] + arrived
    late = call(
        load_kernel,
        jax.ShapeDtypeStruct((width - early_rows, columns), BF16),
        [ANY],
        "load_expert",
        scratch=[pltpu.SemaphoreType.DMA],
        limit=4,
        moved=2 * (width - early_rows) * columns * 2,
    )(piece)
    *arrived, late = lax.optimization_barrier((*arrived, late))
    sums = call(
        sum_kernel,
        jax.ShapeDtypeStruct((rows_here, columns_here), F32),
        [VMEM] * planes,
        "sum_planes",
    )(*arrived)
    sums = lax.all_gather(sums, "group", axis=0, tiled=True)

    resid_out, outgoing = call(
        functools.partial(
            dispatch_kernel, groups, slot_cap, tensor_copies, pieces_each, copies
        ),
        [
            jax.ShapeDtypeStruct((tok_dev, width), BF16),
            jax.ShapeDtypeStruct((tensors * slot_cap, width), BF16),
        ],
        [VMEM] * 6,
        "norm_dispatch",
        scratch=[pltpu.VMEM((rows_here, width), F32)],
    )(
        names,
        jnp.asarray(earlier, BF16),
        jnp.asarray(source, BF16),
        gain,
        resid_all,
        sums,
    )
    rows = lax.all_to_all(
        outgoing.reshape(tensors, slot_cap, width),
        "tensor",
        split_axis=0,
        concat_axis=0,
        tiled=True,
    )
    hidden = call(
        expert_kernel,
        jax.ShapeDtypeStruct((tensors * slot_cap, columns // 2), BF16),
        [VMEM] * 3,
        "experts",
        limit=16,
    )(rows.reshape(tensors * slot_cap, width), early, late)
    return (resid_out[None], hidden.reshape(1, tensors, slot_cap, columns // 2))


def solution(mesh):
    placed = (
        P("group", "tensor", None),
        P("group", None, "tensor"),
        P("group", "tensor", None),
        P("group", "tensor", None),
        P("group", "tensor"),
        P("group", None),
        P("tensor"),
        P("tensor", None),
        P(),
        P("tensor", None, None),
        P(("group", "tensor"), None, None),
    )
    return jax.shard_map(
        local,
        mesh=mesh,
        in_specs=placed,
        out_specs=(P("group", "tensor", None), P(("group", "tensor"), None, None, None)),
        check_vma=False,
    )
```
